32 devices in a mesh: lon: 8 (over y, x, core), lat: 4 (over z).
Axes of the slice: x: 2, y: 2, z: 4, core: 2. Of those that a mesh axis runs over, the one named last changes fastest.
Arguments:
- depth_init: float32 [1024, 1024], P('lat', 'lon'), may hold values from 0.5 to 2.5
- ground: float32 [1024, 1024], P('lat', 'lon'), may hold values from -4 to 4
- roughness: float32 [1024, 1024], P('lat', 'lon'), may hold values from 0.02 to 0.12
- river_init: float32 [1024, 1024], P('lat', 'lon'), may hold values from 0.5 to 4.5
- reach_mask: int32 [1024, 8], P('lat', 'lon'), may hold values from 0 to 1, as said below
- width_class: int32 [1024, 1024], P('lat', 'lon'), may hold values from 0 to 7
- bank_class: int32 [1024, 1024], P('lat', 'lon'), may hold values from 0 to 7
Outputs:
- flood_depth: float32 [1024, 1024], P('lat', 'lon')
- river_depth: float32 [1024, 1024], P('lat', 'lon')
- flow_east: float32 [1024, 1024], P('lat', 'lon')
- flow_north: float32 [1024, 1024], P('lat', 'lon')
The draws below stay inside these ranges and needn't reach their ends.
Inputs may be any that keep to these rules, and one draw needn't show every extreme that they name: Call the 256 rows of one lat index and one lon index of reach_mask a tile. A tile has at most 64 channelled reaches, and some tile exactly 64. A tile with more than 32 has 34 or more, and lies four or more lon indices (around the cycle) from any other such tile of the same lat index; every other tile has at most 16, and some tile beside a full one exactly that many.
All inputs are finite; a program needn't handle non-finite values.
Results may differ from the reference program's by a relative error of at most 0.00002.
Values sent between devices are 32-bit elements; how exact they have to be, the bound alone decides.
No kernel may reach another device: no remote copies, remote signals or barrier semaphores. Data moves between devices by JAX's collectives and lax.ppermute only.
A program may use at most 64 MiB of HBM per device.

```python
import math
import jax
import jax.numpy as jnp

REACH = 128
CY = 256
SUB = 8
STEPS = 4
NY = 1024
NX = 1024
N_LON = 8
N_LAT = 4


def draw_reach_mask(key, part):
    most_slots = CY // 4
    home_slots = CY // 8
    spare_slots = CY // 16
    subkeys = jax.random.split(jax.random.fold_in(key, 17), 3)
    lon_number = jnp.arange(N_LON)[None, :]
    lat_number = jnp.arange(N_LAT)[:, None]
    crowded = (lon_number + lat_number) % 4 == 0
    loaded_count = jax.random.randint(subkeys[0], (N_LAT, N_LON), home_slots + 2, most_slots + 1)
    sparse_count = jax.random.randint(subkeys[1], (N_LAT, N_LON), 0, home_slots - spare_slots + 1)
    counts = jnp.where(crowded, loaded_count, sparse_count)
    counts = counts.at[0, 0].set(most_slots).at[0, 1].set(home_slots - spare_slots)
    scores = jax.random.randint(subkeys[2], (N_LAT, N_LON, CY), 0, 1 << 20) * CY + jnp.arange(CY)[None, None, :]
    row_ranks = jnp.argsort(jnp.argsort(scores, axis=-1), axis=-1)
    chosen = (row_ranks < counts[:, :, None]).astype(jnp.int32)
    return jnp.transpose(chosen, (0, 2, 1)).reshape(N_LAT * CY, N_LON)


def place_ends(entries, stream_key, smallest, top_value):
    shape = entries.shape
    spot = [jax.random.randint(jax.random.fold_in(stream_key, axis), (), 0, shape[axis]) for axis in range(len(shape))]
    entries = entries.at[tuple(spot)].set(smallest)
    longest = shape.index(max(shape))
    spot[longest] = (spot[longest] + 1) % shape[longest]
    return entries.at[tuple(spot)].set(top_value)


def levels(key, extent, shards, low, largest):
    def one(position, blocks):
        heights = jax.random.uniform(jax.random.fold_in(jax.random.fold_in(key, 6), position), (blocks,), jnp.float32, low / len(shards), largest / len(shards))
        return jnp.repeat(jnp.exp(heights), extent[position] // blocks).reshape((-1,) + (1,) * (len(extent) - position - 1))

    level = one(*shards[0])
    for cut in shards[1:]:
        level = level * one(*cut)
    return level


def noise(key, shape, scale, limit, pieces=(), held_as=jnp.bfloat16):
    level = levels(key, shape, pieces, -0.22, 0.18) if pieces else 1.0
    array = jax.random.normal(key, shape, jnp.float32) * scale * level
    return jnp.minimum(jnp.maximum(array, -limit), limit).astype(held_as)


def setup_inputs(seed: int = 0) -> dict:
    arg_keys = jax.random.split(jax.random.key(seed), 8)
    depth_init = jnp.clip(0.5 + 2.0 * jax.random.uniform(arg_keys[0], (NY, NX), jnp.float32) ** levels(arg_keys[0], (NY, NX), ((0, 4), (1, 8)), -0.2, 0.2), 0.5, 2.5)
    ground = noise(arg_keys[1], (NY, NX), 1.0, 4.0, ((0, 4), (1, 8)), jnp.float32)
    roughness = jnp.clip(jnp.exp(math.log(0.12) - 1.7917595 * jax.random.uniform(arg_keys[2], (NY, NX), jnp.float32) ** levels(arg_keys[2], (NY, NX), ((0, 4), (1, 8)), -0.2, 0.2)), 0.02, 0.12)
    river_init = jnp.clip(0.5 + 4.0 * jax.random.uniform(arg_keys[3], (NY, NX), jnp.float32) ** levels(arg_keys[3], (NY, NX), ((0, 4), (1, 8)), -0.2, 0.2), 0.5, 4.5)
    reach_mask = draw_reach_mask(jax.random.fold_in(arg_keys[7], 71), 0)
    width_class = place_ends(jax.random.randint(arg_keys[5], (NY, NX), 0, 8), jax.random.fold_in(arg_keys[5], 1), 0, 7).astype(jnp.int32)
    bank_class = place_ends(jax.random.randint(arg_keys[6], (NY, NX), 0, 8), jax.random.fold_in(arg_keys[6], 1), 0, 7).astype(jnp.int32)
    return {"depth_init": depth_init, "ground": ground, "roughness": roughness, "river_init": river_init, "reach_mask": reach_mask, "width_class": width_class, "bank_class": bank_class}


GRAVITY = 9.81
CELL_SIZE = 90.0
TIME_STEP = 10.0
SHALLOW = 0.1
EXCHANGE = 0.01
CHANNEL_MANNING = 0.035


def face_flow(current, surface_from, surface_to, ground_from, ground_to, friction, breadth, duration):
    height = jnp.maximum(surface_from, surface_to) - jnp.maximum(ground_from, ground_to)
    driven = current - GRAVITY * duration * breadth * height * (surface_to - surface_from) / CELL_SIZE
    resisted = 1.0 + GRAVITY * duration * friction * jnp.abs(current) / (height * height + SHALLOW * SHALLOW) ** (7.0 / 6.0)
    return driven / resisted


def reach_update(river_bed, channel_width, safe_width, river_depth, discharge, surface):
    duration = TIME_STEP / SUB
    breadth = 0.5 * (channel_width[:, :-1] + channel_width[:, 1:])
    safe_breadth = 0.5 * (safe_width[:, :-1] + safe_width[:, 1:])
    friction = CHANNEL_MANNING * CHANNEL_MANNING / safe_breadth
    closed = jnp.zeros_like(river_depth[:, :1])
    gathered = jnp.zeros_like(river_depth)
    for substep in range(SUB):
        water_level = river_bed + river_depth
        interior = face_flow(discharge[:, :-1], water_level[:, :-1], water_level[:, 1:], river_bed[:, :-1], river_bed[:, 1:], friction, breadth, duration)
        discharge = jnp.concatenate([interior, closed], axis=1)
        inflow = jnp.concatenate([closed, interior], axis=1)
        transfer = EXCHANGE * (water_level - surface)
        river_depth = river_depth + duration * ((inflow - discharge) / (safe_width * CELL_SIZE) - transfer)
        gathered = gathered + duration * transfer
    return river_depth, discharge, gathered


def reference(depth_init, ground, roughness, river_init, reach_mask, width_class, bank_class):
    row_count, col_count = ground.shape
    channel_width = 8.0 + 9.0 * width_class.astype(jnp.float32)
    river_bed = ground - (1.0 + 0.5 * bank_class.astype(jnp.float32))
    channelled = jnp.repeat(reach_mask, REACH, axis=1) > 0
    open_north = (jnp.arange(row_count) < row_count - 1)[:, None]

    def as_reaches(field):
        return field.reshape(row_count * N_LON, REACH)

    def as_cells(field):
        return field.reshape(row_count, col_count)

    flood = depth_init
    river_depth = river_init
    discharge = jnp.zeros((row_count, col_count), jnp.float32)
    flow_east = jnp.zeros((row_count, col_count), jnp.float32)
    flow_north = jnp.zeros((row_count, col_count), jnp.float32)
    zero_row = jnp.zeros((1, col_count), jnp.float32)
    for repeat in range(STEPS):
        surface = ground + flood
        flow_east = face_flow(flow_east, surface, jnp.roll(surface, -1, 1), ground, jnp.roll(ground, -1, 1),
                              roughness * jnp.roll(roughness, -1, 1), 1.0, TIME_STEP)
        north_flux = face_flow(flow_north, surface, jnp.roll(surface, -1, 0), ground, jnp.roll(ground, -1, 0),
                               roughness * jnp.roll(roughness, -1, 0), 1.0, TIME_STEP)
        flow_north = jnp.where(open_north, north_flux, 0.0)
        from_west = jnp.roll(flow_east, 1, 1)
        from_south = jnp.concatenate([zero_row, flow_north[:-1]], axis=0)
        flooded = flood + TIME_STEP / CELL_SIZE * (from_west - flow_east + from_south - flow_north)
        new_river, new_discharge, gathered = reach_update(
            as_reaches(river_bed), as_reaches(channel_width), as_reaches(channel_width),
            as_reaches(river_depth), as_reaches(discharge), as_reaches(surface))
        flood = flooded + jnp.where(channelled, as_cells(gathered) * channel_width / CELL_SIZE, 0.0)
        river_depth = jnp.where(channelled, as_cells(new_river), river_depth)
        discharge = jnp.where(channelled, as_cells(new_discharge), discharge)
    return flood, river_depth, flow_east, flow_north
```

```python
import jax
import jax.numpy as jnp
from jax import lax
from jax.experimental import pallas as pl
from jax.experimental.pallas import tpu as pltpu
from jax.sharding import PartitionSpec as P

SUB = 8
STEPS = 4

GRAVITY = 9.81
CELL_SIZE = 90.0
TIME_STEP = 10.0
SHALLOW = 0.1
EXCHANGE = 0.01
CHANNEL_MANNING = 0.035

RIM = 8
COLS = SUB * (STEPS - 2)
DURATION = TIME_STEP / SUB
SURFACE, GROUND, ROUGH = range(3)
FLOOD_FIELDS = 3
LEVEL, FLUX, BED, WIDTH, GAIN, LIVE = range(6)
SLOT_FIELDS = 6


def lanes(shape):
    return lax.broadcasted_iota(jnp.int32, shape, 1)


def sublanes(shape):
    return lax.broadcasted_iota(jnp.int32, shape, 0)


def east_of(field):
    return pltpu.roll(field, field.shape[1] - 1, 1)


def power(field, exponent):
    return jnp.exp(jnp.log(field) * exponent)


def face(flow, here, there, top, drive, friction):
    height = jnp.maximum(here, there) - top
    driven = flow - drive * height * (there - here)
    spread = power(height * height + SHALLOW * SHALLOW, -7.0 / 6.0)
    resisted = 1.0 + friction * jnp.abs(flow) * spread
    return driven * pl.reciprocal(resisted, approx=True)


def first_face(here, there, top, drive):
    height = jnp.maximum(here, there) - top
    return -(drive * height * (there - here))


def reach_constants(bed, width):
    top = jnp.maximum(bed, east_of(bed))
    breadth = 0.5 * (width + east_of(width))
    inner = lanes(bed.shape) < bed.shape[1] - 1
    drive = jnp.where(inner, (GRAVITY * DURATION / CELL_SIZE) * breadth, 0.0)
    friction = jnp.where(
        inner, (GRAVITY * DURATION * CHANNEL_MANNING * CHANNEL_MANNING) / breadth, 0.0
    )
    feed = (DURATION / CELL_SIZE) / width
    return top, drive, friction, feed


def reach_substeps(level, flux, surface, constants, starting):
    top, drive, friction, feed = constants
    gathered = None
    for substep in range(SUB):
        there = east_of(level)
        if starting and substep == 0:
            flux = first_face(level, there, top, drive)
        else:
            flux = face(flux, level, there, top, drive, friction)
        transfer = (EXCHANGE * DURATION) * (level - surface)
        level = level + ((pltpu.roll(flux, 1, 1) - flux) * feed - transfer)
        gathered = transfer if gathered is None else gathered + transfer
    return level, flux, gathered


def odd_position(axis):
    return lax.rem(lax.axis_index(axis), 2)


def rows_kernel(mask_hbm, *refs):
    fields, outs, (reals, classes, mask_ref, sems) = refs[:6], refs[6:8], refs[8:]
    rows = mask_hbm.shape[0]
    northern = odd_position("lat") == 0
    copies = [pltpu.make_async_copy(mask_hbm, mask_ref, sems.at[0])]
    for k, field in enumerate(fields):
        for side, start in enumerate((0, rows - RIM)):
            to = reals.at[side, k] if k < 4 else classes.at[side, k - 4]
            copies.append(
                pltpu.make_async_copy(field.at[pl.ds(start, RIM)], to, sems.at[1 + 2 * k + side])
            )
    for copy in copies:
        copy.start()
    for copy in copies:
        copy.wait()
    shape = reals.shape[2:]
    row = sublanes(shape)

    def rims(side, start):
        depth, ground, rough, river = [reals[side, k] for k in range(4)]
        width, bank = classes[side, 0], classes[side, 1]
        live = jnp.zeros(shape, jnp.float32)
        for j in range(RIM):
            live = jnp.where(row == j, mask_ref[start + j].astype(jnp.float32), live)
        bed = ground - (1.0 + 0.5 * bank.astype(jnp.float32))
        wide = 8.0 + 9.0 * width.astype(jnp.float32)
        return [ground + depth, ground, rough, bed + river, bed, wide, live]

    for k, (low, high) in enumerate(zip(rims(0, 0), rims(1, rows - RIM))):
        outs[0][RIM * k : RIM * (k + 1), :] = jnp.where(northern, high, low)
        outs[1][RIM * k : RIM * (k + 1), :] = jnp.where(northern, low, high)


def fill_list(mask_ref, rows_ref):
    rows, room = mask_ref.shape[0], rows_ref.shape[0]
    for i in range(room):
        rows_ref[i] = rows + 2 * RIM
    count = jnp.int32(0)
    batch = 16
    for r in range(0, rows, batch):
        bits = [mask_ref[r + j] for j in range(batch)]
        places = []
        for j in range(batch):
            places.append(count)
            count = count + bits[j]
        for j in range(batch):
            rows_ref[places[j]] = r + j + RIM
    rows_ref[count] = rows + 2 * RIM


def first_reaches(slot_ref, t):
    at = slice(t, t + RIM)
    width = slot_ref[WIDTH, at, :]
    constants = reach_constants(slot_ref[BED, at, :], width)
    level, flux, gathered = reach_substeps(
        slot_ref[LEVEL, at, :], None, slot_ref[GAIN, at, :], constants, True
    )
    slot_ref[LEVEL, at, :] = level
    slot_ref[FLUX, at, :] = flux
    live = slot_ref[LIVE, at, :] > 0.0
    slot_ref[GAIN, at, :] = jnp.where(live, gathered * (width / CELL_SIZE), 0.0)


def own_kernel(
    mask_ref, depth_ref, ground_ref, river_ref, width_ref, bank_ref,
    rows_ref, slot_ref, surface_ref, gain_ref, level_ref, listed_ref,
    bed_ref, wide_ref,
):
    rows, cols = depth_ref.shape
    slots = rows // 4
    tail = rows + RIM
    fill_list(mask_ref, rows_ref)
    ground = ground_ref[...]
    bed = ground - (1.0 + 0.5 * bank_ref[...].astype(jnp.float32))
    surface_ref[RIM:tail, :] = ground + depth_ref[...]
    surface_ref[tail + RIM : tail + 2 * RIM, :] = jnp.zeros((RIM, cols), jnp.float32)
    level_ref[0:rows, :] = bed + river_ref[...]
    bed_ref[0:rows, :] = bed
    wide_ref[0:rows, :] = 8.0 + 9.0 * width_ref[...].astype(jnp.float32)
    level_ref[rows : rows + RIM, :] = jnp.zeros((RIM, cols), jnp.float32)
    bed_ref[rows : rows + RIM, :] = jnp.zeros((RIM, cols), jnp.float32)
    wide_ref[rows : rows + RIM, :] = jnp.ones((RIM, cols), jnp.float32)
    gain_ref[...] = jnp.zeros(gain_ref.shape, jnp.float32)
    lane = lanes((RIM, cols))
    listed = jnp.zeros((RIM, cols), jnp.float32)

    for i in range(slots):
        e = rows_ref[i]
        own = jnp.where(e < tail, e - RIM, rows)
        to, of, surf = pl.ds(i, 1), pl.ds(own, 1), pl.ds(e, 1)
        slot_ref[LEVEL, to, :] = level_ref[of, :]
        slot_ref[BED, to, :] = bed_ref[of, :]
        slot_ref[WIDTH, to, :] = wide_ref[of, :]
        slot_ref[GAIN, to, :] = surface_ref[surf, :]
        occupied = jnp.where(e < tail, 1.0, 0.0)
        slot_ref[LIVE, to, :] = jnp.full((1, cols), occupied, jnp.float32)
        listed = jnp.where(lane == cols - slots + i, e.astype(jnp.float32), listed)
    listed_ref[...] = listed
    for t in range(0, slots, RIM):
        first_reaches(slot_ref, t)
    for i in range(slots):
        gain_ref[pl.ds(rows_ref[i], 1), :] = slot_ref[GAIN, pl.ds(i, 1), :]


def pack_kernel(
    ground_ref, rough_ref, own_slot, surface_ref, own_gain, listed_ref, p_ref, q_ref,
    a_ref, b_ref, flood_ref, slot_ref, gain_ref,
):
    rows, cols = ground_ref.shape
    slots = rows // 4
    tail = rows + RIM
    half = RIM // 2
    northern = odd_position("lat") == 0
    p, q = p_ref[...], q_ref[...]
    north = jnp.where(northern, p, q)
    south = jnp.where(northern, q, p)

    def rim(block, k):
        return block[RIM * k : RIM * (k + 1)]

    def ends(k):
        return jnp.concatenate([rim(south, k)[half:], rim(north, k)[:half]], axis=0)

    last = slice(slots, slots + RIM)
    slot_ref[GAIN, last, :] = ends(0)
    slot_ref[LEVEL, last, :] = ends(3)
    slot_ref[BED, last, :] = ends(4)
    slot_ref[WIDTH, last, :] = ends(5)
    slot_ref[LIVE, last, :] = ends(6)
    first_reaches(slot_ref, slots)
    slot_ref[:, 0:slots, :] = own_slot[:, 0:slots, :]
    flood_ref[SURFACE, RIM:tail, :] = surface_ref[RIM:tail, :]
    flood_ref[GROUND, RIM:tail, :] = ground_ref[...]
    flood_ref[ROUGH, RIM:tail, :] = rough_ref[...]
    for k in range(FLOOD_FIELDS):
        flood_ref[k, 0:RIM, :] = rim(south, k)
        flood_ref[k, tail : tail + RIM, :] = rim(north, k)
        flood_ref[k, tail + RIM : tail + 2 * RIM, :] = jnp.zeros((RIM, cols), jnp.float32)
    gain_ref[...] = own_gain[...]
    gain_ref[half:RIM, :] = slot_ref[GAIN, slots : slots + half, :]
    gain_ref[tail : tail + half, :] = slot_ref[GAIN, slots + half : slots + RIM, :]

    groups = cols // COLS
    group = lanes((RIM, cols)) // COLS
    eastern = odd_position("lon") == 0
    from_a = jnp.where(eastern, cols - COLS, 0)
    from_b = jnp.where(eastern, 0, cols - COLS)
    tiles = []
    for k in range(FLOOD_FIELDS):
        for t in range(0, rows + 2 * RIM, RIM):
            tiles.append((flood_ref, k, t))
    for k in range(SLOT_FIELDS):
        for t in range(0, slots + RIM, RIM):
            tiles.append((slot_ref, k, t))
    listed = listed_ref[...]
    for out_ref, start in ((a_ref, from_a), (b_ref, from_b)):
        for m in range(0, len(tiles), groups):
            block = listed
            for g, (ref, k, t) in enumerate(tiles[m : m + groups]):
                source = ref[k, t : t + RIM, :]
                moved = pltpu.roll(source, lax.rem(cols + COLS * g - start, cols), 1)
                block = jnp.where(group == g, moved, block)
            out_ref[m // groups * RIM : (m // groups + 1) * RIM, :] = block


def step_kernel(
    rows_ref, flood_ref, slot_ref, gain_ref, level_ref, bank_ref, a_ref, b_ref,
    depth_out, river_out, east_out, north_out,
    own_ref, side_ref, side_slot, surf_ref, side_gain, own_gain,
    flow_ref, fixed_ref, river_ref, west_rows, east_rows, sems,
):
    rows, cols = depth_out.shape
    slots = rows // 4
    tail = rows + RIM
    ext = rows + 2 * RIM
    total = slots + RIM
    half = RIM // 2
    lat_number, lat_total = lax.axis_index("lat"), lax.axis_size("lat")
    eastern = odd_position("lon") == 0
    lists = a_ref.shape[0] - RIM

    def fetch(to_a, to_b):
        one = pltpu.make_async_copy(a_ref.at[lists], to_a, sems.at[0])
        two = pltpu.make_async_copy(b_ref.at[lists], to_b, sems.at[1])
        return one, two

    one, two = fetch(east_rows, west_rows)
    one.start()
    two.start()

    groups = cols // COLS
    lane = lanes((RIM, cols))
    low = lane < cols // 2
    use_a = (lane < cols // 2) == eastern
    to_a = jnp.where(eastern, 0, cols - COLS)
    to_b = jnp.where(eastern, cols - COLS, 0)
    tiles = []
    for k in range(FLOOD_FIELDS):
        for t in range(0, ext, RIM):
            tiles.append((side_ref, k, t))
    for k in range(SLOT_FIELDS):
        for t in range(0, total, RIM):
            tiles.append((side_slot, k, t))
    for n, (ref, k, t) in enumerate(tiles):
        m, g = n // groups, n % groups
        at = slice(m * RIM, (m + 1) * RIM)
        from_a = pltpu.roll(a_ref[at, :], lax.rem(cols + to_a - COLS * g, cols), 1)
        from_b = pltpu.roll(b_ref[at, :], lax.rem(cols + to_b - COLS * g, cols), 1)
        ref[k, t : t + RIM, :] = jnp.where(use_a, from_a, from_b)
    for t in range(0, ext + RIM, RIM):
        own_ref[t : t + RIM, :] = flood_ref[SURFACE, t : t + RIM, :]
        own_gain[t : t + RIM, :] = gain_ref[t : t + RIM, :]
        for k in range(2):
            side_gain[k, t : t + RIM, :] = jnp.zeros((RIM, cols), jnp.float32)
    side_ref[SURFACE, ext : ext + RIM, :] = jnp.zeros((RIM, cols), jnp.float32)
    one.wait()
    two.wait()

    first = cols - slots

    def east_row(i):
        return jnp.where(eastern, east_rows[first + i], west_rows[first + i]).astype(jnp.int32)

    def west_row(i):
        return jnp.where(eastern, west_rows[first + i], east_rows[first + i]).astype(jnp.int32)

    def spread_side():
        for i in range(slots):
            line = side_slot[GAIN, pl.ds(i, 1), :]
            side_gain[0, pl.ds(east_row(i), 1), :] = line
            side_gain[1, pl.ds(west_row(i), 1), :] = line
        for k in range(2):
            side_gain[k, half:RIM, :] = side_slot[GAIN, slots : slots + half, :]
            side_gain[k, tail : tail + half, :] = side_slot[GAIN, slots + half : total, :]

    def spread_own():
        for i in range(slots):
            own_gain[pl.ds(rows_ref[i], 1), :] = slot_ref[GAIN, pl.ds(i, 1), :]
        own_gain[half:RIM, :] = slot_ref[GAIN, slots : slots + half, :]
        own_gain[tail : tail + half, :] = slot_ref[GAIN, slots + half : total, :]

    spread_side()

    def reaches(state, surface, t):
        at = slice(t, t + RIM)
        width = state[WIDTH, at, :]
        constants = reach_constants(state[BED, at, :], width)
        level, flux, gathered = reach_substeps(
            state[LEVEL, at, :], state[FLUX, at, :], surface[at, :], constants, False
        )
        state[LEVEL, at, :] = level
        state[FLUX, at, :] = flux
        live = state[LIVE, at, :] > 0.0
        state[GAIN, at, :] = jnp.where(live, gathered * (width / CELL_SIZE), 0.0)

    last_lane = lane == cols - 1
    first_lane = lane == 0
    row = sublanes((RIM, cols))
    first_row, last_row = row == 0, row == RIM - 1
    drive = GRAVITY * TIME_STEP / CELL_SIZE
    share = TIME_STEP / CELL_SIZE

    def pair_east(own, side):
        a, b = east_of(own), east_of(side)
        return jnp.where(last_lane, b, a), jnp.where(last_lane, a, b)

    def pair_west(own, side):
        a, b = pltpu.roll(own, 1, 1), pltpu.roll(side, 1, 1)
        return jnp.where(first_lane, b, a), jnp.where(first_lane, a, b)

    def constants_of(t):
        at = slice(t, t + RIM)
        up = slice(t + 1, t + 1 + RIM)
        ground = flood_ref[GROUND, at, :], side_ref[GROUND, at, :]
        rough = flood_ref[ROUGH, at, :], side_ref[ROUGH, at, :]
        ground_east, rough_east = pair_east(*ground), pair_east(*rough)
        weight = GRAVITY * TIME_STEP
        for j, ref in enumerate((flood_ref, side_ref)):
            fixed_ref[j, 0, at, :] = jnp.maximum(ground[j], ground_east[j])
            fixed_ref[j, 1, at, :] = weight * (rough[j] * rough_east[j])
            fixed_ref[j, 2, at, :] = jnp.maximum(ground[j], ref[GROUND, up, :])
            fixed_ref[j, 3, at, :] = weight * (rough[j] * ref[ROUGH, up, :])

    def flood_step(step):
        before = [None, None]
        for t in range(0, ext, RIM):
            at = slice(t, t + RIM)
            up = slice(t + 1, t + 1 + RIM)
            final = step == STEPS - 1
            if final and t > rows:
                continue
            here = [own_ref[at, :], side_ref[SURFACE, at, :]]
            east = pair_east(*here)
            north = [own_ref[up, :], side_ref[SURFACE, up, :]]
            flows_east, flows_north = [], []
            for j in range(2):
                top_east, top_north = fixed_ref[j, 0, at, :], fixed_ref[j, 2, at, :]
                if step == 0:
                    to_east = first_face(here[j], east[j], top_east, drive)
                    to_north = first_face(here[j], north[j], top_north, drive)
                else:
                    to_east = face(
                        flow_ref[j, 0, at, :], here[j], east[j], top_east, drive, fixed_ref[j, 1, at, :]
                    )
                    to_north = None
                    if j == 0 or not final:
                        to_north = face(
                            flow_ref[j, 1, at, :], here[j], north[j], top_north, drive,
                            fixed_ref[j, 3, at, :],
                        )
                if to_north is not None and t == 0:
                    to_north = jnp.where(last_row & (lat_number == 0), 0.0, to_north)
                if to_north is not None and t == rows:
                    to_north = jnp.where(last_row & (lat_number == lat_total - 1), 0.0, to_north)
                flows_east.append(to_east)
                flows_north.append(to_north)
                if not final:
                    flow_ref[j, 0, at, :] = to_east
                    flow_ref[j, 1, at, :] = to_north
            west = pair_west(*flows_east)
            for j in range(1 if final else 2):
                turned = pltpu.roll(flows_north[j], 1, 0)
                under = turned if before[j] is None else before[j]
                south = jnp.where(first_row, under, turned)
                before[j] = turned
                moved = share * (west[j] - flows_east[j] + south - flows_north[j])
                if j == 0:
                    new = here[j] + moved + own_gain[at, :]
                    if not final:
                        own_ref[at, :] = new
                    elif t > 0:
                        out = slice(t - RIM, t)
                        depth_out[out, :] = new - flood_ref[GROUND, at, :]
                        east_out[out, :] = flows_east[0]
                        north_out[out, :] = flows_north[0]
                else:
                    gain = jnp.where(low, side_gain[0, at, :], side_gain[1, at, :])
                    side_ref[SURFACE, at, :] = here[j] + moved + gain

    for t in range(0, ext, RIM):
        constants_of(t)
    flood_step(0)
    for step in range(1, STEPS):
        for i in range(slots):
            surf_ref[0, pl.ds(i, 1), :] = own_ref[pl.ds(rows_ref[i], 1), :]
        surf_ref[0, slots : slots + half, :] = own_ref[half:RIM, :]
        surf_ref[0, slots + half : total, :] = own_ref[tail : tail + half, :]
        for t in range(0, total, RIM):
            reaches(slot_ref, surf_ref.at[0], t)
        spread_own()
        if step < STEPS - 1:
            middle = lanes((1, cols)) < cols // 2
            for i in range(slots):
                surf_ref[1, pl.ds(i, 1), :] = jnp.where(
                    middle,
                    side_ref[SURFACE, pl.ds(east_row(i), 1), :],
                    side_ref[SURFACE, pl.ds(west_row(i), 1), :],
                )
            surf_ref[1, slots : slots + half, :] = side_ref[SURFACE, half:RIM, :]
            surf_ref[1, slots + half : total, :] = side_ref[SURFACE, tail : tail + half, :]
            for t in range(0, total, RIM):
                reaches(side_slot, surf_ref.at[1], t)
            spread_side()
        flood_step(step)
    river_ref[0:rows, :] = level_ref[0:rows, :]
    for i in range(slots):
        e = rows_ref[i]
        own = jnp.where(e < tail, e - RIM, rows)
        river_ref[pl.ds(own, 1), :] = slot_ref[LEVEL, pl.ds(i, 1), :]
    bed = flood_ref[GROUND, RIM:tail, :] - (1.0 + 0.5 * bank_ref[...].astype(jnp.float32))
    river_out[...] = river_ref[0:rows, :] - bed


def swaps(count, first):
    pairs = [(i, i + 1) for i in range(first, count - 1, 2)]
    return pairs + [(b, a) for a, b in pairs]


def body(depth_init, ground, roughness, river_init, reach_mask, width_class, bank_class):
    rows, cols = ground.shape
    slots = rows // 4
    f32 = jnp.float32
    lon_total, lat_total = lax.axis_size("lon"), lax.axis_size("lat")
    mask = reach_mask.reshape(rows)
    smem = pl.BlockSpec(memory_space=pltpu.SMEM)
    vmem = pl.BlockSpec(memory_space=pltpu.VMEM)
    fields = (depth_init, ground, roughness, river_init, width_class, bank_class)
    ext = rows + 2 * RIM
    params = pltpu.CompilerParams(vmem_limit_bytes=48 * 1024 * 1024)

    hbm = pl.BlockSpec(memory_space=pltpu.HBM)
    rim_shape = jax.ShapeDtypeStruct((7 * RIM, cols), f32)
    to_p, to_q = pl.pallas_call(
        rows_kernel,
        in_specs=[hbm] * 7,
        out_specs=[vmem, vmem],
        out_shape=[rim_shape, rim_shape],
        scratch_shapes=[
            pltpu.VMEM((2, 4, RIM, cols), f32),
            pltpu.VMEM((2, 2, RIM, cols), jnp.int32),
            pltpu.SMEM((rows,), jnp.int32),
            pltpu.SemaphoreType.DMA((13,)),
        ],
        compiler_params=pltpu.CompilerParams(vmem_limit_bytes=63 * 1024 * 1024),
        name="rims",
    )(mask, *fields)
    got_p = lax.ppermute(to_p, "lat", swaps(lat_total, 0))
    got_q = lax.ppermute(to_q, "lat", swaps(lat_total, 1))
    slot_shape = jax.ShapeDtypeStruct((SLOT_FIELDS, slots + RIM, cols), f32)
    dense = jax.ShapeDtypeStruct((ext + RIM, cols), f32)
    row_list, own_slot, surface, own_gain, level, listed = pl.pallas_call(
        own_kernel,
        in_specs=[smem] + [vmem] * 5,
        out_specs=[smem] + [vmem] * 5,
        out_shape=[
            jax.ShapeDtypeStruct((2 * slots,), jnp.int32),
            slot_shape,
            dense,
            dense,
            jax.ShapeDtypeStruct((rows + RIM, cols), f32),
            jax.ShapeDtypeStruct((RIM, cols), f32),
        ],
        scratch_shapes=[pltpu.VMEM((rows + RIM, cols), f32)] * 2,
        compiler_params=params,
        name="own_reaches",
    )(mask, depth_init, ground, river_init, width_class, bank_class)

    tiles = FLOOD_FIELDS * ext // RIM + SLOT_FIELDS * (slots // RIM + 1)
    message = -(-(tiles + slots // COLS) // (cols // COLS)) * RIM
    message_shape = jax.ShapeDtypeStruct((message, cols), f32)
    to_a, to_b, flood, slot, gain = pl.pallas_call(
        pack_kernel,
        in_specs=[vmem] * 8,
        out_specs=[vmem] * 5,
        out_shape=[
            message_shape,
            message_shape,
            jax.ShapeDtypeStruct((FLOOD_FIELDS, ext + RIM, cols), f32),
            slot_shape,
            dense,
        ],
        compiler_params=params,
        name="pack",
    )(ground, roughness, own_slot, surface, own_gain, listed, got_p, got_q)
    ring = swaps(lon_total, 1) + [(lon_total - 1, 0), (0, lon_total - 1)]
    got_a = lax.ppermute(to_a, "lon", swaps(lon_total, 0))
    got_b = lax.ppermute(to_b, "lon", ring)

    tile = jax.ShapeDtypeStruct((rows, cols), f32)
    return pl.pallas_call(
        step_kernel,
        in_specs=[smem] + [vmem] * 7,
        out_specs=[vmem] * 4,
        out_shape=[tile] * 4,
        scratch_shapes=[
            pltpu.VMEM((ext + RIM, cols), f32),
            pltpu.VMEM((FLOOD_FIELDS, ext + RIM, cols), f32),
            pltpu.VMEM((SLOT_FIELDS, slots + RIM, cols), f32),
            pltpu.VMEM((2, slots + RIM, cols), f32),
            pltpu.VMEM((2, ext + RIM, cols), f32),
            pltpu.VMEM((ext + RIM, cols), f32),
            pltpu.VMEM((2, 2, ext, cols), f32),
            pltpu.VMEM((2, 4, ext, cols), f32),
            pltpu.VMEM((rows + RIM, cols), f32),
            pltpu.SMEM((cols,), f32),
            pltpu.SMEM((cols,), f32),
            pltpu.SemaphoreType.DMA((2,)),
        ],
        compiler_params=params,
        name="steps",
    )(row_list, flood, slot, gain, level, bank_class, got_a, got_b)


def solution(mesh):
    grid = P("lat", "lon")
    return jax.shard_map(
        body,
        mesh=mesh,
        in_specs=(grid,) * 7,
        out_specs=(grid,) * 4,
        check_vma=False,
    )
```

```python
import jax
import jax.numpy as jnp
from jax import lax
from jax.experimental import pallas as pl
from jax.experimental.pallas import tpu as pltpu
from jax.sharding import PartitionSpec as P

SUB = 8
STEPS = 4

GRAVITY = 9.81
CELL_SIZE = 90.0
TIME_STEP = 10.0
SHALLOW = 0.1
EXCHANGE = 0.01
CHANNEL_MANNING = 0.035

RIM = 8
COLS = SUB * (STEPS - 2)
DURATION = TIME_STEP / SUB
SURFACE, GROUND, ROUGH = range(3)
FLOOD_FIELDS = 3
LEVEL, FLUX, BED, WIDTH, GAIN, LIVE = range(6)
SLOT_FIELDS = 6
TOP, DRIVE, FRICTION, FEED, WATER = range(6, 11)
BATCH = 72
ROWS_AT_ONCE = 64
TILES_AT_ONCE = 34
FLOOD_AT_ONCE = 34
UNPACK_AT_ONCE = 20
SUBS_AT_ONCE = 8
FIRST_AT_ONCE = 7


def lanes(shape):
    return lax.broadcasted_iota(jnp.int32, shape, 1)


def sublanes(shape):
    return lax.broadcasted_iota(jnp.int32, shape, 0)


def east_of(field):
    return pltpu.roll(field, field.shape[1] - 1, 1)


def face(flow, here, there, top, drive, friction):
    height = jnp.maximum(here, there) - top
    driven = flow - drive * height * (there - here)
    spread = jnp.exp(jnp.log(height * height + SHALLOW * SHALLOW) * (-7.0 / 6.0))
    resisted = 1.0 + friction * jnp.abs(flow) * spread
    return driven * pl.reciprocal(resisted, approx=True)


def first_face(here, there, top, drive):
    height = jnp.maximum(here, there) - top
    return -(drive * height * (there - here))


def reach_constants(bed, width):
    top = jnp.maximum(bed, east_of(bed))
    breadth = 0.5 * (width + east_of(width))
    inner = lanes(bed.shape) < bed.shape[1] - 1
    drive = jnp.where(inner, (GRAVITY * DURATION / CELL_SIZE) * breadth, 0.0)
    friction = jnp.where(
        inner, (GRAVITY * DURATION * CHANNEL_MANNING * CHANNEL_MANNING) / breadth, 0.0
    )
    feed = (DURATION / CELL_SIZE) / width
    return top, drive, friction, feed


def west_of(field):
    return pltpu.roll(field, 1, 1)


def advanced(level, west, flux, surface, feed):
    transfer = (EXCHANGE * DURATION) * (level - surface)
    return level + ((west - flux) * feed - transfer), transfer


def first_reaches(level, surface, constants):
    top, drive, friction, feed = constants
    west_faces = [west_of(value) for value in (top, drive, friction)]
    flux = first_face(level, east_of(level), top, drive)
    west = first_face(west_of(level), level, west_faces[0], west_faces[1])
    level, gathered = advanced(level, west, flux, surface, feed)

    def substep(_, state):
        level, west, flux, gathered = state
        west = face(west, west_of(level), level, *west_faces)
        flux = face(flux, level, east_of(level), top, drive, friction)
        level, transfer = advanced(level, west, flux, surface, feed)
        return level, west, flux, gathered + transfer

    state = repeated(SUB - 1, FIRST_AT_ONCE, substep, (level, west, flux, gathered))
    return state[0], state[2], state[3]


def odd_position(axis):
    return lax.rem(lax.axis_index(axis), 2)


def repeated(count, unroll, step, carry):
    if unroll >= count:
        for i in range(count):
            carry = step(i, carry)
        return carry

    def some(block, carry):
        for j in range(unroll):
            carry = step(block * unroll + j, carry)
        return carry

    return lax.fori_loop(0, count // unroll, some, carry)


def each_row(count, visit, unroll=ROWS_AT_ONCE):
    repeated(count, unroll, lambda i, carry: (visit(i), carry)[1], 0)


def row_of(tile):
    return tile * RIM if isinstance(tile, int) else pl.multiple_of(tile * RIM, RIM)


def each_tile(count, visit, unroll):
    repeated(count, unroll, lambda i, carry: (visit(row_of(i)), carry)[1], 0)


def rows_kernel(mask_hbm, *refs):
    fields, outs, (reals, classes, mask_ref, sems) = refs[:6], refs[6:8], refs[8:]
    rows = mask_hbm.shape[0]
    northern = odd_position("lat") == 0
    copies = [pltpu.make_async_copy(mask_hbm, mask_ref, sems.at[0])]
    for k, field in enumerate(fields):
        for side, start in enumerate((0, rows - RIM)):
            to = reals.at[side, k] if k < 4 else classes.at[side, k - 4]
            copies.append(
                pltpu.make_async_copy(field.at[pl.ds(start, RIM)], to, sems.at[1 + 2 * k + side])
            )
    for copy in copies:
        copy.start()
    for copy in copies:
        copy.wait()
    shape = reals.shape[2:]
    row = sublanes(shape)

    def rims(side, start):
        depth, ground, rough, river = [reals[side, k] for k in range(4)]
        width, bank = classes[side, 0], classes[side, 1]
        live = jnp.zeros(shape, jnp.float32)
        for j in range(RIM):
            live = jnp.where(row == j, mask_ref[start + j].astype(jnp.float32), live)
        bed = ground - (1.0 + 0.5 * bank.astype(jnp.float32))
        wide = 8.0 + 9.0 * width.astype(jnp.float32)
        return [ground + depth, ground, rough, bed + river, bed, wide, live]

    for k, (low, high) in enumerate(zip(rims(0, 0), rims(1, rows - RIM))):
        outs[0][RIM * k : RIM * (k + 1), :] = jnp.where(northern, high, low)
        outs[1][RIM * k : RIM * (k + 1), :] = jnp.where(northern, low, high)


def fill_list(mask_ref, rows_ref):
    rows, room = mask_ref.shape[0], rows_ref.shape[0]
    beyond = rows + 2 * RIM
    batch = 16

    def clear(i):
        rows_ref[i] = beyond

    each_row(room, clear, 16)

    def enter(block, count):
        first = block * batch
        bits = [mask_ref[first + j] for j in range(batch)]
        places = []
        for bit in bits:
            places.append(count)
            count = count + bit
        for j, place in enumerate(places):
            rows_ref[place] = first + (j + RIM)
        return count

    count = lax.fori_loop(0, rows // batch, enter, jnp.int32(0))
    rows_ref[count] = beyond


def own_kernel(
    mask_ref, depth_ref, ground_ref, rough_ref, river_ref, width_ref, bank_ref,
    rows_ref, flat_ref, gain_ref, level_ref, listed_ref,
    bed_ref, wide_ref,
):
    rows, cols = depth_ref.shape
    slots = rows // 4
    tail, ext, total = rows + RIM, rows + 2 * RIM, slots + RIM
    base = FLOOD_FIELDS * ext
    fill_list(mask_ref, rows_ref)

    def prepare(t):
        at = pl.ds(t, RIM)
        ground = ground_ref[at, :]
        bed = ground - (1.0 + 0.5 * bank_ref[at, :].astype(jnp.float32))
        flat_ref[pl.ds(t + (SURFACE * ext + RIM), RIM), :] = ground + depth_ref[at, :]
        flat_ref[pl.ds(t + (GROUND * ext + RIM), RIM), :] = ground
        flat_ref[pl.ds(t + (ROUGH * ext + RIM), RIM), :] = rough_ref[at, :]
        level_ref[at, :] = bed + river_ref[at, :]
        bed_ref[at, :] = bed
        wide_ref[at, :] = 8.0 + 9.0 * width_ref[at, :].astype(jnp.float32)
        gain_ref[at, :] = jnp.zeros((RIM, cols), jnp.float32)

    each_tile(rows // RIM, prepare, TILES_AT_ONCE)
    zero = jnp.zeros((RIM, cols), jnp.float32)
    for t in range(rows, ext + RIM, RIM):
        gain_ref[t : t + RIM, :] = zero
    level_ref[rows:tail, :] = zero
    bed_ref[rows:tail, :] = zero
    wide_ref[rows:tail, :] = zero + 1.0
    lane = lanes((RIM, cols))

    def gather(i):
        e = rows_ref[i]
        own = e - RIM
        listed_ref[...] = jnp.where(lane == cols - slots + i, e.astype(jnp.float32), listed_ref[...])
        to = base + i
        live = jnp.where(own < rows, 1.0, 0.0)
        own = jnp.minimum(own, rows)
        flat_ref[pl.ds(to + LEVEL * total, 1), :] = level_ref[pl.ds(own, 1), :]
        flat_ref[pl.ds(to + BED * total, 1), :] = bed_ref[pl.ds(own, 1), :]
        flat_ref[pl.ds(to + WIDTH * total, 1), :] = wide_ref[pl.ds(own, 1), :]
        flat_ref[pl.ds(to + LIVE * total, 1), :] = jnp.full((1, cols), live, jnp.float32)
        surface = jnp.minimum(own, rows - 1) + (SURFACE * ext + RIM)
        flat_ref[pl.ds(to + GAIN * total, 1), :] = flat_ref[pl.ds(surface, 1), :]

    listed_ref[...] = zero
    each_row(slots, gather)

    def part(field):
        return slice(base + field * total, base + field * total + slots)

    width = flat_ref[part(WIDTH), :]
    level, flux, gathered = first_reaches(
        flat_ref[part(LEVEL), :],
        flat_ref[part(GAIN), :],
        reach_constants(flat_ref[part(BED), :], width),
    )
    flat_ref[part(LEVEL), :] = level
    flat_ref[part(FLUX), :] = flux
    live = flat_ref[part(LIVE), :] > 0.0
    flat_ref[part(GAIN), :] = jnp.where(live, gathered * (width / CELL_SIZE), 0.0)

    def spread(i):
        gain_ref[pl.ds(rows_ref[i], 1), :] = flat_ref[pl.ds(base + GAIN * total + i, 1), :]

    each_row(slots, spread)


def pack_kernel(
    own_flat, own_gain, listed_ref, p_ref, q_ref,
    flat_ref, gain_ref, a_ref, b_ref,
):
    del own_flat, own_gain
    cols = a_ref.shape[1]
    ext = gain_ref.shape[0] - RIM
    rows = ext - 2 * RIM
    slots = rows // 4
    tail, total = rows + RIM, slots + RIM
    base = FLOOD_FIELDS * ext
    half = RIM // 2
    northern = odd_position("lat") == 0
    p, q = p_ref[...], q_ref[...]
    north = jnp.where(northern, p, q)
    south = jnp.where(northern, q, p)

    def rim(block, k):
        return block[RIM * k : RIM * (k + 1)]

    def ends(k):
        return jnp.concatenate([rim(south, k)[half:], rim(north, k)[:half]], axis=0)

    def part(field):
        start = base + field * total + slots
        return slice(start, start + RIM)

    bed, width = ends(4), ends(5)
    level, flux, gathered = first_reaches(ends(3), ends(0), reach_constants(bed, width))
    gained = jnp.where(ends(6) > 0.0, gathered * (width / CELL_SIZE), 0.0)
    for field, value in (
        (LEVEL, level), (FLUX, flux), (BED, bed), (WIDTH, width), (GAIN, gained), (LIVE, ends(6)),
    ):
        flat_ref[part(field), :] = value
    for k in range(FLOOD_FIELDS):
        flat_ref[k * ext : k * ext + RIM, :] = rim(south, k)
        flat_ref[k * ext + tail : (k + 1) * ext, :] = rim(north, k)
    gain_ref[half:RIM, :] = gained[:half]
    gain_ref[tail : tail + half, :] = gained[half:]

    groups = cols // COLS
    group = lanes((RIM, cols)) // COLS
    eastern = odd_position("lon") == 0
    tiles = (base + SLOT_FIELDS * total) // RIM
    turns = []
    for start in (jnp.where(eastern, cols - COLS, 0), jnp.where(eastern, 0, cols - COLS)):
        turns.append([lax.rem(cols + COLS * g - start, cols) for g in range(groups)])

    def pack(m, used):
        block_a = block_b = listed_ref[...]
        for g in range(used):
            source = flat_ref[pl.ds(row_of(m * groups + g), RIM), :]
            block_a = jnp.where(group == g, pltpu.roll(source, turns[0][g], 1), block_a)
            block_b = jnp.where(group == g, pltpu.roll(source, turns[1][g], 1), block_b)
        to = pl.ds(row_of(m), RIM)
        a_ref[to, :] = block_a
        b_ref[to, :] = block_b

    each_row(tiles // groups, lambda m: pack(m, groups), UNPACK_AT_ONCE)
    pack(tiles // groups, tiles % groups)


def step_kernel(
    rows_ref, flat_ref, gain_ref, level_ref, bank_ref, a_ref, b_ref,
    depth_out, river_out, east_out, north_out,
    own_ref, side_ref, state, side_gain, own_gain,
    flow_ref, fixed_ref, river_ref, list_rows, west_rows, east_rows, sems,
):
    rows, cols = depth_out.shape
    slots = rows // 4
    tail, ext, total = rows + RIM, rows + 2 * RIM, slots + RIM
    base = FLOOD_FIELDS * ext
    half = RIM // 2
    lat_number, lat_total = lax.axis_index("lat"), lax.axis_size("lat")
    eastern = odd_position("lon") == 0
    lists = a_ref.shape[0] - RIM
    zero = jnp.zeros((RIM, cols), jnp.float32)

    list_a, list_b = a_ref[lists : lists + RIM, :], b_ref[lists : lists + RIM, :]
    list_rows[0] = jnp.where(eastern, list_a, list_b).astype(jnp.int32)
    list_rows[1] = jnp.where(eastern, list_b, list_a).astype(jnp.int32)
    one = pltpu.make_async_copy(list_rows.at[0, 0], east_rows, sems.at[0])
    two = pltpu.make_async_copy(list_rows.at[1, 0], west_rows, sems.at[1])
    one.start()
    two.start()

    groups = cols // COLS
    lane = lanes((RIM, cols))
    low = lane < cols // 2
    use_a = low == eastern
    turns = []
    for to in (jnp.where(eastern, 0, cols - COLS), jnp.where(eastern, cols - COLS, 0)):
        turns.append([lax.rem(cols + to - COLS * g, cols) for g in range(groups)])

    def unpack(m):
        at = pl.ds(row_of(m), RIM)
        block_a, block_b = a_ref[at, :], b_ref[at, :]
        for g in range(groups):
            from_a = pltpu.roll(block_a, turns[0][g], 1)
            from_b = pltpu.roll(block_b, turns[1][g], 1)
            to = pl.ds(row_of(m * groups + g), RIM)
            side_ref[to, :] = jnp.where(use_a, from_a, from_b)

    each_row(a_ref.shape[0] // RIM, unpack, UNPACK_AT_ONCE)

    def copy_in(t):
        at = pl.ds(t, RIM)
        own_ref[at, :] = flat_ref[at, :]
        own_gain[at, :] = gain_ref[at, :]
        for k in range(2):
            side_gain[k, at, :] = zero

    each_tile(ext // RIM, copy_in, TILES_AT_ONCE)
    own_ref[ext : ext + RIM, :] = zero

    def copy_slots(t):
        values = []
        for field in range(SLOT_FIELDS):
            own = flat_ref[pl.ds(base + field * total + t, RIM), :]
            side = side_ref[pl.ds(base + field * total + t, RIM), :]
            state[field, pl.ds(t, RIM), :] = own
            state[field, pl.ds(total + t, RIM), :] = side
            values.append((own, side))
        for j in range(2):
            constants = reach_constants(values[BED][j], values[WIDTH][j])
            for field, value in zip((TOP, DRIVE, FRICTION, FEED), constants):
                state[field, pl.ds(j * total + t, RIM), :] = value

    each_tile(total // RIM, copy_slots, TILES_AT_ONCE)
    one.wait()
    two.wait()
    first = cols - slots

    def spread_side():
        def visit(i):
            line = state[GAIN, pl.ds(total + i, 1), :]
            side_gain[0, pl.ds(east_rows[first + i], 1), :] = line
            side_gain[1, pl.ds(west_rows[first + i], 1), :] = line

        each_row(slots, visit)
        start = total + slots
        for k in range(2):
            side_gain[k, half:RIM, :] = state[GAIN, start : start + half, :]
            side_gain[k, tail : tail + half, :] = state[GAIN, start + half : start + RIM, :]

    def spread_own():
        def visit(i):
            own_gain[pl.ds(rows_ref[i], 1), :] = state[GAIN, pl.ds(i, 1), :]

        each_row(slots, visit)
        own_gain[half:RIM, :] = state[GAIN, slots : slots + half, :]
        own_gain[tail : tail + half, :] = state[GAIN, slots + half : total, :]

    spread_side()

    def reaches(start, size):
        at = slice(start, start + size)

        faces = [state[k, at, :] for k in (TOP, DRIVE, FRICTION)]
        west_faces = [west_of(value) for value in faces]
        surface, feed = state[WATER, at, :], state[FEED, at, :]

        def substep(_, carry):
            level, west, flux, gathered = carry
            west = face(west, west_of(level), level, *west_faces)
            flux = face(flux, level, east_of(level), *faces)
            level, transfer = advanced(level, west, flux, surface, feed)
            return level, west, flux, gathered + transfer

        level, flux = state[LEVEL, at, :], state[FLUX, at, :]
        start = (level, west_of(flux), flux, jnp.zeros_like(level))
        level, _, flux, gathered = repeated(SUB, SUBS_AT_ONCE, substep, start)
        state[LEVEL, at, :] = level
        state[FLUX, at, :] = flux
        live = state[LIVE, at, :] > 0.0
        state[GAIN, at, :] = jnp.where(live, gathered * (state[WIDTH, at, :] / CELL_SIZE), 0.0)

    last_lane = lane == cols - 1
    first_lane = lane == 0
    row = sublanes((RIM, cols))
    first_row = row == 0
    drive = GRAVITY * TIME_STEP / CELL_SIZE
    share = TIME_STEP / CELL_SIZE
    edge_south = jnp.where(lat_number == 0, RIM - 1, -1)
    edge_north = jnp.where(lat_number == lat_total - 1, tail - 1, -1)

    def pair_east(own, side):
        a, b = east_of(own), east_of(side)
        return jnp.where(last_lane, b, a), jnp.where(last_lane, a, b)

    def pair_west(own, side):
        a, b = pltpu.roll(own, 1, 1), pltpu.roll(side, 1, 1)
        return jnp.where(first_lane, b, a), jnp.where(first_lane, a, b)

    def constants_of(t):
        at = pl.ds(t, RIM)

        def read(field, shift):
            where = pl.ds(t + (field * ext + shift), RIM)
            return flat_ref[where, :], side_ref[where, :]

        ground, rough = read(GROUND, 0), read(ROUGH, 0)
        ground_north, rough_north = read(GROUND, 1), read(ROUGH, 1)
        ground_east, rough_east = pair_east(*ground), pair_east(*rough)
        weight = GRAVITY * TIME_STEP
        for j in range(2):
            fixed_ref[j, 0, at, :] = jnp.maximum(ground[j], ground_east[j])
            fixed_ref[j, 1, at, :] = weight * (rough[j] * rough_east[j])
            fixed_ref[j, 2, at, :] = jnp.maximum(ground[j], ground_north[j])
            fixed_ref[j, 3, at, :] = weight * (rough[j] * rough_north[j])

    def north_flow(j, t, here, step):
        at = pl.ds(t, RIM)
        north = (own_ref, side_ref)[j][pl.ds(t + 1, RIM), :]
        top = fixed_ref[j, 2, at, :]
        if step == 0:
            flow = first_face(here, north, top, drive)
        else:
            flow = face(flow_ref[j, 1, at, :], here, north, top, drive, fixed_ref[j, 3, at, :])
        e = t + row
        return jnp.where((e == edge_south) | (e == edge_north), 0.0, flow)

    def flood_tile(t, before, step):
        at = pl.ds(t, RIM)
        final = step == STEPS - 1
        here = own_ref[at, :], side_ref[at, :]
        east = pair_east(*here)
        to_east = []
        for j in range(2):
            top = fixed_ref[j, 0, at, :]
            if step == 0:
                flow = first_face(here[j], east[j], top, drive)
            else:
                flow = face(
                    flow_ref[j, 0, at, :], here[j], east[j], top, drive, fixed_ref[j, 1, at, :]
                )
            to_east.append(flow)
        west = pair_west(*to_east)
        after = []
        for j in range(1 if final else 2):
            to_north = north_flow(j, t, here[j], step)
            turned = pltpu.roll(to_north, 1, 0)
            south = jnp.where(first_row, before[j], turned)
            after.append(turned)
            new = here[j] + share * (west[j] - to_east[j] + south - to_north)
            if final:
                out = pl.ds(t - RIM, RIM)
                new = new + own_gain[at, :]
                depth_out[out, :] = new - flat_ref[pl.ds(t + GROUND * ext, RIM), :]
                east_out[out, :] = to_east[0]
                north_out[out, :] = to_north
                continue
            flow_ref[j, 0, at, :] = to_east[j]
            flow_ref[j, 1, at, :] = to_north
            if j == 0:
                own_ref[at, :] = new + own_gain[at, :]
            else:
                side_ref[at, :] = new + jnp.where(low, side_gain[0, at, :], side_gain[1, at, :])
        return tuple(after)

    def flood_step(step, tiles):
        final = step == STEPS - 1
        begin, count = (1, rows // RIM) if final else (0, ext // RIM)
        before = (zero, zero)
        if final:
            before = (pltpu.roll(north_flow(0, 0, own_ref[0:RIM, :], step), 1, 0),)

        repeated(count, tiles, lambda i, before: flood_tile(row_of(i + begin), before, step), before)

    each_tile(ext // RIM, constants_of, TILES_AT_ONCE)
    flood_step(0, FLOOD_AT_ONCE)
    middle = lanes((1, cols)) < cols // 2
    for step in range(1, STEPS):
        sides = step < STEPS - 1

        def water(i):
            state[WATER, pl.ds(i, 1), :] = own_ref[pl.ds(rows_ref[i], 1), :]
            if sides:
                state[WATER, pl.ds(total + i, 1), :] = jnp.where(
                    middle,
                    side_ref[pl.ds(east_rows[first + i], 1), :],
                    side_ref[pl.ds(west_rows[first + i], 1), :],
                )

        each_row(slots, water)
        for j, ref in enumerate((own_ref, side_ref)[: 2 if sides else 1]):
            start = j * total + slots
            state[WATER, start : start + half, :] = ref[half:RIM, :]
            state[WATER, start + half : start + RIM, :] = ref[tail : tail + half, :]
        for start in range(0, (2 if sides else 1) * total, BATCH):
            reaches(start, BATCH)
        spread_own()
        if sides:
            spread_side()
        flood_step(step, FLOOD_AT_ONCE)

    river_ref[0:rows, :] = level_ref[0:rows, :]

    def settle(i):
        own = jnp.minimum(rows_ref[i] - RIM, rows)
        river_ref[pl.ds(own, 1), :] = state[LEVEL, pl.ds(i, 1), :]

    each_row(slots, settle)

    def finish(t):
        at = pl.ds(t, RIM)
        ground = flat_ref[pl.ds(t + (GROUND * ext + RIM), RIM), :]
        bed = ground - (1.0 + 0.5 * bank_ref[at, :].astype(jnp.float32))
        river_out[at, :] = river_ref[at, :] - bed

    each_tile(rows // RIM, finish, TILES_AT_ONCE)


def swaps(count, first):
    pairs = [(i, i + 1) for i in range(first, count - 1, 2)]
    return pairs + [(b, a) for a, b in pairs]


def body(depth_init, ground, roughness, river_init, reach_mask, width_class, bank_class):
    rows, cols = ground.shape
    slots = rows // 4
    f32 = jnp.float32
    lon_total, lat_total = lax.axis_size("lon"), lax.axis_size("lat")
    mask = reach_mask.reshape(rows)
    smem = pl.BlockSpec(memory_space=pltpu.SMEM)
    vmem = pl.BlockSpec(memory_space=pltpu.VMEM)
    fields = (depth_init, ground, roughness, river_init, width_class, bank_class)
    ext, total = rows + 2 * RIM, slots + RIM
    used = FLOOD_FIELDS * ext + SLOT_FIELDS * total
    groups = cols // COLS
    message = -(-(used // RIM + slots // COLS) // groups) * RIM
    room = message * groups
    params = pltpu.CompilerParams(vmem_limit_bytes=48 * 1024 * 1024)

    hbm = pl.BlockSpec(memory_space=pltpu.HBM)
    rim_shape = jax.ShapeDtypeStruct((7 * RIM, cols), f32)
    to_p, to_q = pl.pallas_call(
        rows_kernel,
        in_specs=[hbm] * 7,
        out_specs=[vmem, vmem],
        out_shape=[rim_shape, rim_shape],
        scratch_shapes=[
            pltpu.VMEM((2, 4, RIM, cols), f32),
            pltpu.VMEM((2, 2, RIM, cols), jnp.int32),
            pltpu.SMEM((rows,), jnp.int32),
            pltpu.SemaphoreType.DMA((13,)),
        ],
        compiler_params=pltpu.CompilerParams(vmem_limit_bytes=63 * 1024 * 1024),
        name="rims",
    )(mask, *fields)
    got_q = lax.ppermute(to_q, "lat", swaps(lat_total, 1))
    got_p = lax.ppermute(to_p, "lat", swaps(lat_total, 0))
    flat_shape = jax.ShapeDtypeStruct((room, cols), f32)
    dense = jax.ShapeDtypeStruct((ext + RIM, cols), f32)
    row_list, own_flat, own_gain, level, listed = pl.pallas_call(
        own_kernel,
        in_specs=[smem] + [vmem] * 6,
        out_specs=[smem] + [vmem] * 4,
        out_shape=[
            jax.ShapeDtypeStruct((2 * slots,), jnp.int32),
            flat_shape,
            dense,
            jax.ShapeDtypeStruct((rows + RIM, cols), f32),
            jax.ShapeDtypeStruct((RIM, cols), f32),
        ],
        scratch_shapes=[pltpu.VMEM((rows + RIM, cols), f32)] * 2,
        compiler_params=params,
        name="own_reaches",
    )(mask, *fields)

    message_shape = jax.ShapeDtypeStruct((message, cols), f32)
    flat, gain, to_a, to_b = pl.pallas_call(
        pack_kernel,
        in_specs=[vmem] * 5,
        out_specs=[vmem] * 4,
        out_shape=[flat_shape, dense, message_shape, message_shape],
        input_output_aliases={0: 0, 1: 1},
        compiler_params=params,
        name="pack",
    )(own_flat, own_gain, listed, got_p, got_q)
    ring = swaps(lon_total, 1) + [(lon_total - 1, 0), (0, lon_total - 1)]
    got_a = lax.ppermute(to_a, "lon", swaps(lon_total, 0))
    got_b = lax.ppermute(to_b, "lon", ring)

    tile = jax.ShapeDtypeStruct((rows, cols), f32)
    return pl.pallas_call(
        step_kernel,
        in_specs=[smem] + [vmem] * 6,
        out_specs=[vmem] * 4,
        out_shape=[tile] * 4,
        scratch_shapes=[
            pltpu.VMEM((ext + RIM, cols), f32),
            pltpu.VMEM((room, cols), f32),
            pltpu.VMEM((WATER + 1, 2 * total, cols), f32),
            pltpu.VMEM((2, ext + RIM, cols), f32),
            pltpu.VMEM((ext + RIM, cols), f32),
            pltpu.VMEM((2, 2, ext, cols), f32),
            pltpu.VMEM((2, 4, ext, cols), f32),
            pltpu.VMEM((rows + RIM, cols), f32),
            pltpu.VMEM((2, RIM, cols), jnp.int32),
            pltpu.SMEM((cols,), jnp.int32),
            pltpu.SMEM((cols,), jnp.int32),
            pltpu.SemaphoreType.DMA((2,)),
        ],
        compiler_params=params,
        name="steps",
    )(row_list, flat, gain, level, bank_class, got_a, got_b)


def solution(mesh):
    grid = P("lat", "lon")
    return jax.shard_map(
        body,
        mesh=mesh,
        in_specs=(grid,) * 7,
        out_specs=(grid,) * 4,
        check_vma=False,
    )
```

```python
import jax
import jax.numpy as jnp
from jax import lax
from jax.experimental import pallas as pl
from jax.experimental.pallas import tpu as pltpu
from jax.sharding import PartitionSpec as P

SUB = 8
STEPS = 4

GRAVITY = 9.81
CELL_SIZE = 90.0
TIME_STEP = 10.0
SHALLOW = 0.1
EXCHANGE = 0.01
CHANNEL_MANNING = 0.035

RIM = 8
COLS = SUB * (STEPS - 2)
DURATION = TIME_STEP / SUB
SURFACE, GROUND, ROUGH = range(3)
FLOOD_FIELDS = 3
LEVEL, FLUX, BED, WIDTH, GAIN, LIVE = range(6)
SLOT_FIELDS = 6
TOP, DRIVE, FRICTION, FEED, WATER = range(6, 11)
ROWS_AT_ONCE = 64
TILES_AT_ONCE = 34
UNPACK_AT_ONCE = 20
FIRST_AT_ONCE = 7


def lanes(shape):
    return lax.broadcasted_iota(jnp.int32, shape, 1)


def sublanes(shape):
    return lax.broadcasted_iota(jnp.int32, shape, 0)


def east_of(field):
    return pltpu.roll(field, field.shape[1] - 1, 1)


def face(flow, here, there, top, drive, friction):
    height = jnp.maximum(here, there) - top
    driven = flow - drive * height * (there - here)
    spread = jnp.exp(jnp.log(height * height + SHALLOW * SHALLOW) * (-7.0 / 6.0))
    resisted = 1.0 + friction * jnp.abs(flow) * spread
    return driven * pl.reciprocal(resisted, approx=True)


def first_face(here, there, top, drive):
    height = jnp.maximum(here, there) - top
    return -(drive * height * (there - here))


def reach_constants(bed, width):
    top = jnp.maximum(bed, east_of(bed))
    breadth = 0.5 * (width + east_of(width))
    inner = lanes(bed.shape) < bed.shape[1] - 1
    drive = jnp.where(inner, (GRAVITY * DURATION / CELL_SIZE) * breadth, 0.0)
    friction = jnp.where(
        inner, (GRAVITY * DURATION * CHANNEL_MANNING * CHANNEL_MANNING) / breadth, 0.0
    )
    feed = (DURATION / CELL_SIZE) / width
    return top, drive, friction, feed


def west_of(field):
    return pltpu.roll(field, 1, 1)


def advanced(level, west, flux, surface, feed):
    transfer = (EXCHANGE * DURATION) * (level - surface)
    return level + ((west - flux) * feed - transfer), transfer


def first_reaches(level, surface, constants):
    top, drive, friction, feed = constants
    west_faces = [west_of(value) for value in (top, drive, friction)]
    flux = first_face(level, east_of(level), top, drive)
    west = first_face(west_of(level), level, west_faces[0], west_faces[1])
    level, gathered = advanced(level, west, flux, surface, feed)

    def substep(_, state):
        level, west, flux, gathered = state
        west = face(west, west_of(level), level, *west_faces)
        flux = face(flux, level, east_of(level), top, drive, friction)
        level, transfer = advanced(level, west, flux, surface, feed)
        return level, west, flux, gathered + transfer

    state = repeated(SUB - 1, FIRST_AT_ONCE, substep, (level, west, flux, gathered))
    return state[0], state[2], state[3]


def odd_position(axis):
    return lax.rem(lax.axis_index(axis), 2)


def repeated(count, unroll, step, carry):
    if unroll >= count:
        for i in range(count):
            carry = step(i, carry)
        return carry

    def some(block, carry):
        for j in range(unroll):
            carry = step(block * unroll + j, carry)
        return carry

    return lax.fori_loop(0, count // unroll, some, carry)


def each_row(count, visit, unroll=ROWS_AT_ONCE):
    repeated(count, unroll, lambda i, carry: (visit(i), carry)[1], 0)


def row_of(tile):
    return tile * RIM if isinstance(tile, int) else pl.multiple_of(tile * RIM, RIM)


def each_tile(count, visit, unroll):
    repeated(count, unroll, lambda i, carry: (visit(row_of(i)), carry)[1], 0)


def rows_kernel(mask_hbm, *refs):
    fields, outs, (reals, classes, mask_ref, sems) = refs[:6], refs[6:8], refs[8:]
    rows = mask_hbm.shape[0]
    northern = odd_position("lat") == 0
    copies = [pltpu.make_async_copy(mask_hbm, mask_ref, sems.at[0])]
    for k, field in enumerate(fields):
        for side, start in enumerate((0, rows - RIM)):
            to = reals.at[side, k] if k < 4 else classes.at[side, k - 4]
            copies.append(
                pltpu.make_async_copy(field.at[pl.ds(start, RIM)], to, sems.at[1 + 2 * k + side])
            )
    for copy in copies:
        copy.start()
    for copy in copies:
        copy.wait()
    shape = reals.shape[2:]
    row = sublanes(shape)

    def rims(side, start):
        depth, ground, rough, river = [reals[side, k] for k in range(4)]
        width, bank = classes[side, 0], classes[side, 1]
        live = jnp.zeros(shape, jnp.float32)
        for j in range(RIM):
            live = jnp.where(row == j, mask_ref[start + j].astype(jnp.float32), live)
        bed = ground - (1.0 + 0.5 * bank.astype(jnp.float32))
        wide = 8.0 + 9.0 * width.astype(jnp.float32)
        return [ground + depth, ground, rough, bed + river, bed, wide, live]

    for k, (low, high) in enumerate(zip(rims(0, 0), rims(1, rows - RIM))):
        outs[0][RIM * k : RIM * (k + 1), :] = jnp.where(northern, high, low)
        outs[1][RIM * k : RIM * (k + 1), :] = jnp.where(northern, low, high)


def fill_list(mask_ref, rows_ref):
    rows = mask_ref.shape[0]
    room = rows // 4
    beyond = rows + 2 * RIM
    batch = 16

    for i in range(room):
        rows_ref[i] = beyond
    count = jnp.int32(0)
    for first in range(0, rows, batch):
        bits = [mask_ref[first + j] for j in range(batch)]
        places = []
        for bit in bits:
            places.append(count)
            count = count + bit
        for j, place in enumerate(places):
            rows_ref[place] = first + j + RIM
    rows_ref[count] = beyond


def own_kernel(
    mask_ref, depth_ref, ground_ref, rough_ref, river_ref, width_ref, bank_ref,
    rows_ref, flat_ref, gain_ref, level_ref, listed_ref,
    bed_ref, wide_ref,
):
    rows, cols = depth_ref.shape
    slots = rows // 4
    tail, ext, total = rows + RIM, rows + 2 * RIM, slots + RIM
    base = FLOOD_FIELDS * ext
    fill_list(mask_ref, rows_ref)

    def prepare(t):
        at = pl.ds(t, RIM)
        ground = ground_ref[at, :]
        bed = ground - (1.0 + 0.5 * bank_ref[at, :].astype(jnp.float32))
        flat_ref[pl.ds(t + (SURFACE * ext + RIM), RIM), :] = ground + depth_ref[at, :]
        flat_ref[pl.ds(t + (GROUND * ext + RIM), RIM), :] = ground
        flat_ref[pl.ds(t + (ROUGH * ext + RIM), RIM), :] = rough_ref[at, :]
        level_ref[at, :] = bed + river_ref[at, :]
        bed_ref[at, :] = bed
        wide_ref[at, :] = 8.0 + 9.0 * width_ref[at, :].astype(jnp.float32)
        gain_ref[at, :] = jnp.zeros((RIM, cols), jnp.float32)

    each_tile(rows // RIM, prepare, TILES_AT_ONCE)
    zero = jnp.zeros((RIM, cols), jnp.float32)
    flat_ref[SURFACE * ext + tail : (SURFACE + 1) * ext, :] = zero
    for t in range(rows, ext + RIM, RIM):
        gain_ref[t : t + RIM, :] = zero
    level_ref[rows:tail, :] = zero
    bed_ref[rows:tail, :] = zero
    wide_ref[rows:tail, :] = zero + 1.0
    lane = lanes((RIM, cols))

    listed = zero
    for i in range(slots):
        e = rows_ref[i]
        own = jnp.minimum(e - RIM, rows)
        listed = jnp.where(lane == cols - slots + i, e.astype(jnp.float32), listed)
        to = base + i
        live = jnp.where(e < tail, 1.0, 0.0)
        of, surface = pl.ds(own, 1), pl.ds(own + (SURFACE * ext + RIM), 1)
        flat_ref[pl.ds(to + LEVEL * total, 1), :] = level_ref[of, :]
        flat_ref[pl.ds(to + BED * total, 1), :] = bed_ref[of, :]
        flat_ref[pl.ds(to + WIDTH * total, 1), :] = wide_ref[of, :]
        flat_ref[pl.ds(to + LIVE * total, 1), :] = jnp.full((1, cols), live, jnp.float32)
        flat_ref[pl.ds(to + GAIN * total, 1), :] = flat_ref[surface, :]
    listed_ref[...] = listed

    def part(field):
        return slice(base + field * total, base + field * total + slots)

    width = flat_ref[part(WIDTH), :]
    level, flux, gathered = first_reaches(
        flat_ref[part(LEVEL), :],
        flat_ref[part(GAIN), :],
        reach_constants(flat_ref[part(BED), :], width),
    )
    flat_ref[part(LEVEL), :] = level
    flat_ref[part(FLUX), :] = flux
    live = flat_ref[part(LIVE), :] > 0.0
    flat_ref[part(GAIN), :] = jnp.where(live, gathered * (width / CELL_SIZE), 0.0)

    def spread(i):
        gain_ref[pl.ds(rows_ref[i], 1), :] = flat_ref[pl.ds(base + GAIN * total + i, 1), :]

    each_row(slots, spread)


def pack_kernel(
    own_flat, own_gain, listed_ref, p_ref, q_ref,
    flat_ref, gain_ref, a_ref, b_ref,
):
    del own_flat, own_gain
    cols = a_ref.shape[1]
    ext = gain_ref.shape[0] - RIM
    rows = ext - 2 * RIM
    slots = rows // 4
    tail, total = rows + RIM, slots + RIM
    base = FLOOD_FIELDS * ext
    half = RIM // 2
    northern = odd_position("lat") == 0
    p, q = p_ref[...], q_ref[...]
    north = jnp.where(northern, p, q)
    south = jnp.where(northern, q, p)

    def rim(block, k):
        return block[RIM * k : RIM * (k + 1)]

    def ends(k):
        return jnp.concatenate([rim(south, k)[half:], rim(north, k)[:half]], axis=0)

    def part(field):
        start = base + field * total + slots
        return slice(start, start + RIM)

    bed, width = ends(4), ends(5)
    level, flux, gathered = first_reaches(ends(3), ends(0), reach_constants(bed, width))
    gained = jnp.where(ends(6) > 0.0, gathered * (width / CELL_SIZE), 0.0)
    for field, value in (
        (LEVEL, level), (FLUX, flux), (BED, bed), (WIDTH, width), (GAIN, gained), (LIVE, ends(6)),
    ):
        flat_ref[part(field), :] = value
    for k in range(FLOOD_FIELDS):
        flat_ref[k * ext : k * ext + RIM, :] = rim(south, k)
        flat_ref[k * ext + tail : (k + 1) * ext, :] = rim(north, k)
    gain_ref[half:RIM, :] = gained[:half]
    gain_ref[tail : tail + half, :] = gained[half:]

    groups = cols // COLS
    group = lanes((RIM, cols)) // COLS
    eastern = odd_position("lon") == 0
    tiles = (base + SLOT_FIELDS * total) // RIM
    turns = []
    for start in (jnp.where(eastern, cols - COLS, 0), jnp.where(eastern, 0, cols - COLS)):
        turns.append([lax.rem(cols + COLS * g - start, cols) for g in range(groups)])

    def pack(m, used):
        block_a = block_b = listed_ref[...]
        for g in range(used):
            source = flat_ref[pl.ds(row_of(m * groups + g), RIM), :]
            block_a = jnp.where(group == g, pltpu.roll(source, turns[0][g], 1), block_a)
            block_b = jnp.where(group == g, pltpu.roll(source, turns[1][g], 1), block_b)
        to = pl.ds(row_of(m), RIM)
        a_ref[to, :] = block_a
        b_ref[to, :] = block_b

    each_row(tiles // groups, lambda m: pack(m, groups), UNPACK_AT_ONCE)
    pack(tiles // groups, tiles % groups)


def step_kernel(
    rows_ref, flat_ref, gain_ref, level_ref, bank_ref, a_ref, b_ref,
    depth_out, river_out, east_out, north_out,
    own_ref, side_ref, state, side_gain, own_gain,
    flow_ref, fixed_ref, river_ref, list_rows, west_rows, east_rows, sems,
):
    rows, cols = depth_out.shape
    slots = rows // 4
    tail, ext, total = rows + RIM, rows + 2 * RIM, slots + RIM
    base = FLOOD_FIELDS * ext
    half = RIM // 2
    lat_number, lat_total = lax.axis_index("lat"), lax.axis_size("lat")
    eastern = odd_position("lon") == 0
    lists = a_ref.shape[0] - RIM
    zero = jnp.zeros((RIM, cols), jnp.float32)

    list_a, list_b = a_ref[lists : lists + RIM, :], b_ref[lists : lists + RIM, :]
    list_rows[0] = jnp.where(eastern, list_a, list_b).astype(jnp.int32)
    list_rows[1] = jnp.where(eastern, list_b, list_a).astype(jnp.int32)
    one = pltpu.make_async_copy(list_rows.at[0, 0], east_rows, sems.at[0])
    two = pltpu.make_async_copy(list_rows.at[1, 0], west_rows, sems.at[1])
    one.start()
    two.start()

    groups = cols // COLS
    lane = lanes((RIM, cols))
    low = lane < cols // 2
    use_a = low == eastern
    turns = []
    for to in (jnp.where(eastern, 0, cols - COLS), jnp.where(eastern, cols - COLS, 0)):
        turns.append([lax.rem(cols + to - COLS * g, cols) for g in range(groups)])

    def unpack(m):
        at = pl.ds(row_of(m), RIM)
        block_a, block_b = a_ref[at, :], b_ref[at, :]
        for g in range(groups):
            from_a = pltpu.roll(block_a, turns[0][g], 1)
            from_b = pltpu.roll(block_b, turns[1][g], 1)
            to = pl.ds(row_of(m * groups + g), RIM)
            side_ref[to, :] = jnp.where(use_a, from_a, from_b)

    each_row(a_ref.shape[0] // RIM, unpack, UNPACK_AT_ONCE)

    def copy_in(t):
        at = pl.ds(t, RIM)
        own_ref[at, :] = flat_ref[at, :]
        own_gain[at, :] = gain_ref[at, :]
        for k in range(2):
            side_gain[k, at, :] = zero

    each_tile(ext // RIM, copy_in, TILES_AT_ONCE)
    own_ref[ext : ext + RIM, :] = zero

    def copy_slots(t):
        values = []
        for field in range(SLOT_FIELDS):
            own = flat_ref[pl.ds(base + field * total + t, RIM), :]
            side = side_ref[pl.ds(base + field * total + t, RIM), :]
            state[field, pl.ds(t, RIM), :] = own
            state[field, pl.ds(total + t, RIM), :] = side
            values.append((own, side))
        for j in range(2):
            constants = reach_constants(values[BED][j], values[WIDTH][j])
            for field, value in zip((TOP, DRIVE, FRICTION, FEED), constants):
                state[field, pl.ds(j * total + t, RIM), :] = value

    each_tile(total // RIM, copy_slots, TILES_AT_ONCE)
    one.wait()
    two.wait()
    first = cols - slots

    def spread_side():
        def visit(i):
            line = state[GAIN, pl.ds(total + i, 1), :]
            side_gain[0, pl.ds(east_rows[first + i], 1), :] = line
            side_gain[1, pl.ds(west_rows[first + i], 1), :] = line

        each_row(slots, visit)
        start = total + slots
        for k in range(2):
            side_gain[k, half:RIM, :] = state[GAIN, start : start + half, :]
            side_gain[k, tail : tail + half, :] = state[GAIN, start + half : start + RIM, :]

    def spread_own():
        def visit(i):
            own_gain[pl.ds(rows_ref[i], 1), :] = state[GAIN, pl.ds(i, 1), :]

        each_row(slots, visit)
        own_gain[half:RIM, :] = state[GAIN, slots : slots + half, :]
        own_gain[tail : tail + half, :] = state[GAIN, slots + half : total, :]

    spread_side()

    def reaches(start, size):
        at = slice(start, start + size)

        faces = [state[k, at, :] for k in (TOP, DRIVE, FRICTION)]
        west_faces = [west_of(value) for value in faces]
        surface, feed = state[WATER, at, :], state[FEED, at, :]

        level, flux = state[LEVEL, at, :], state[FLUX, at, :]
        west, gathered = west_of(flux), jnp.zeros_like(level)
        for _ in range(SUB):
            west = face(west, west_of(level), level, *west_faces)
            flux = face(flux, level, east_of(level), *faces)
            level, transfer = advanced(level, west, flux, surface, feed)
            gathered = gathered + transfer
            yield
        state[LEVEL, at, :] = level
        state[FLUX, at, :] = flux
        live = state[LIVE, at, :] > 0.0
        state[GAIN, at, :] = jnp.where(live, gathered * (state[WIDTH, at, :] / CELL_SIZE), 0.0)

    last_lane = lane == cols - 1
    first_lane = lane == 0
    row = sublanes((RIM, cols))
    first_row = row == 0
    drive = GRAVITY * TIME_STEP / CELL_SIZE
    share = TIME_STEP / CELL_SIZE
    edge_south = jnp.where(lat_number == 0, RIM - 1, -1)
    edge_north = jnp.where(lat_number == lat_total - 1, tail - 1, -1)

    def pair_east(own, side):
        a, b = east_of(own), east_of(side)
        return jnp.where(last_lane, b, a), jnp.where(last_lane, a, b)

    def pair_west(own, side):
        a, b = pltpu.roll(own, 1, 1), pltpu.roll(side, 1, 1)
        return jnp.where(first_lane, b, a), jnp.where(first_lane, a, b)

    def constants_of(t):
        at = pl.ds(t, RIM)

        def read(field, shift):
            where = pl.ds(t + (field * ext + shift), RIM)
            return flat_ref[where, :], side_ref[where, :]

        ground, rough = read(GROUND, 0), read(ROUGH, 0)
        ground_north, rough_north = read(GROUND, 1), read(ROUGH, 1)
        ground_east, rough_east = pair_east(*ground), pair_east(*rough)
        weight = GRAVITY * TIME_STEP
        for j in range(2):
            fixed_ref[j, 0, at, :] = jnp.maximum(ground[j], ground_east[j])
            fixed_ref[j, 1, at, :] = weight * (rough[j] * rough_east[j])
            fixed_ref[j, 2, at, :] = jnp.maximum(ground[j], ground_north[j])
            fixed_ref[j, 3, at, :] = weight * (rough[j] * rough_north[j])

    def north_flow(j, t, here, step):
        at = pl.ds(t, RIM)
        north = (own_ref, side_ref)[j][pl.ds(t + 1, RIM), :]
        top = fixed_ref[j, 2, at, :]
        if step == 0:
            flow = first_face(here, north, top, drive)
        else:
            flow = face(flow_ref[j, 1, at, :], here, north, top, drive, fixed_ref[j, 3, at, :])
        e = t + row
        return jnp.where((e == edge_south) | (e == edge_north), 0.0, flow)

    def flows(t, step):
        at = pl.ds(t, RIM)
        final = step == STEPS - 1
        here = own_ref[at, :], side_ref[at, :]
        for j in range(1 if final else 2):
            flow_ref[j, 1, at, :] = north_flow(j, t, here[j], step)
        if final and t == 0:
            return
        east = pair_east(*here)
        for j in range(2):
            top = fixed_ref[j, 0, at, :]
            if step == 0:
                flow = first_face(here[j], east[j], top, drive)
            else:
                flow = face(
                    flow_ref[j, 0, at, :], here[j], east[j], top, drive, fixed_ref[j, 1, at, :]
                )
            flow_ref[j, 0, at, :] = flow

    def update(t, before, step):
        at = pl.ds(t, RIM)
        final = step == STEPS - 1
        to_east = flow_ref[0, 0, at, :], flow_ref[1, 0, at, :]
        west = pair_west(*to_east)
        after = []
        for j in range(1 if final else 2):
            to_north = flow_ref[j, 1, at, :]
            turned = pltpu.roll(to_north, 1, 0)
            south = jnp.where(first_row, before[j], turned)
            after.append(turned)
            moved = share * (west[j] - to_east[j] + south - to_north)
            if final:
                out = pl.ds(t - RIM, RIM)
                new = own_ref[at, :] + moved + own_gain[at, :]
                depth_out[out, :] = new - flat_ref[pl.ds(t + GROUND * ext, RIM), :]
                east_out[out, :] = to_east[0]
                north_out[out, :] = to_north
            elif j == 0:
                own_ref[at, :] = own_ref[at, :] + moved + own_gain[at, :]
            else:
                gain = jnp.where(low, side_gain[0, at, :], side_gain[1, at, :])
                side_ref[at, :] = side_ref[at, :] + moved + gain
        return after

    def update_all(step):
        if step == STEPS - 1:
            before = (pltpu.roll(flow_ref[0, 1, 0:RIM, :], 1, 0),)
            tiles = range(RIM, tail, RIM)
        else:
            before = (zero, zero)
            tiles = range(0, ext, RIM)
        for t in tiles:
            before = update(t, before, step)

    def settle():
        river_ref[0:rows, :] = level_ref[0:rows, :]
        for i in range(slots):
            own = jnp.minimum(rows_ref[i] - RIM, rows)
            river_ref[pl.ds(own, 1), :] = state[LEVEL, pl.ds(i, 1), :]
        for t in range(0, rows, RIM):
            at = pl.ds(t, RIM)
            ground = flat_ref[pl.ds(t + (GROUND * ext + RIM), RIM), :]
            bed = ground - (1.0 + 0.5 * bank_ref[at, :].astype(jnp.float32))
            river_out[at, :] = river_ref[at, :] - bed

    for t in range(0, ext, RIM):
        constants_of(t)
        flows(t, 0)
    update_all(0)
    middle = lanes((1, cols)) < cols // 2
    for step in range(1, STEPS):
        sides = step < STEPS - 1

        def water(i):
            state[WATER, pl.ds(i, 1), :] = own_ref[pl.ds(rows_ref[i], 1), :]
            if sides:
                state[WATER, pl.ds(total + i, 1), :] = jnp.where(
                    middle,
                    side_ref[pl.ds(east_rows[first + i], 1), :],
                    side_ref[pl.ds(west_rows[first + i], 1), :],
                )

        each_row(slots, water)
        for j, ref in enumerate((own_ref, side_ref)[: 2 if sides else 1]):
            start = j * total + slots
            state[WATER, start : start + half, :] = ref[half:RIM, :]
            state[WATER, start + half : start + RIM, :] = ref[tail : tail + half, :]

        running = [reaches(start, total) for start in range(0, (2 if sides else 1) * total, total)]
        tiles = list(range(0, ext if sides else tail, RIM))
        share_of = -(-len(tiles) // SUB)
        for substep in range(SUB):
            for reach in running:
                next(reach)
            for t in tiles[substep * share_of : (substep + 1) * share_of]:
                flows(t, step)
        for reach in running:
            next(reach, None)
        spread_own()
        if sides:
            spread_side()
        else:
            settle()
        update_all(step)


def swaps(count, first):
    pairs = [(i, i + 1) for i in range(first, count - 1, 2)]
    return pairs + [(b, a) for a, b in pairs]


def body(depth_init, ground, roughness, river_init, reach_mask, width_class, bank_class):
    rows, cols = ground.shape
    slots = rows // 4
    f32 = jnp.float32
    lon_total, lat_total = lax.axis_size("lon"), lax.axis_size("lat")
    mask = reach_mask.reshape(rows)
    smem = pl.BlockSpec(memory_space=pltpu.SMEM)
    vmem = pl.BlockSpec(memory_space=pltpu.VMEM)
    fields = (depth_init, ground, roughness, river_init, width_class, bank_class)
    ext, total = rows + 2 * RIM, slots + RIM
    used = FLOOD_FIELDS * ext + SLOT_FIELDS * total
    groups = cols // COLS
    message = -(-(used // RIM + slots // COLS) // groups) * RIM
    room = message * groups
    params = pltpu.CompilerParams(vmem_limit_bytes=48 * 1024 * 1024)

    hbm = pl.BlockSpec(memory_space=pltpu.HBM)
    rim_shape = jax.ShapeDtypeStruct((7 * RIM, cols), f32)
    to_p, to_q = pl.pallas_call(
        rows_kernel,
        in_specs=[hbm] * 7,
        out_specs=[vmem, vmem],
        out_shape=[rim_shape, rim_shape],
        scratch_shapes=[
            pltpu.VMEM((2, 4, RIM, cols), f32),
            pltpu.VMEM((2, 2, RIM, cols), jnp.int32),
            pltpu.SMEM((rows,), jnp.int32),
            pltpu.SemaphoreType.DMA((13,)),
        ],
        compiler_params=pltpu.CompilerParams(vmem_limit_bytes=63 * 1024 * 1024),
        name="rims",
    )(mask, *fields)
    got_p = lax.ppermute(to_p, "lat", swaps(lat_total, 0))
    got_q = lax.ppermute(to_q, "lat", swaps(lat_total, 1))
    flat_shape = jax.ShapeDtypeStruct((room, cols), f32)
    dense = jax.ShapeDtypeStruct((ext + RIM, cols), f32)
    row_list, own_flat, own_gain, level, listed = pl.pallas_call(
        own_kernel,
        in_specs=[smem] + [vmem] * 6,
        out_specs=[smem] + [vmem] * 4,
        out_shape=[
            jax.ShapeDtypeStruct((2 * slots,), jnp.int32),
            flat_shape,
            dense,
            jax.ShapeDtypeStruct((rows + RIM, cols), f32),
            jax.ShapeDtypeStruct((RIM, cols), f32),
        ],
        scratch_shapes=[pltpu.VMEM((rows + RIM, cols), f32)] * 2,
        compiler_params=params,
        name="own_reaches",
    )(mask, *fields)

    message_shape = jax.ShapeDtypeStruct((message, cols), f32)
    flat, gain, to_a, to_b = pl.pallas_call(
        pack_kernel,
        in_specs=[vmem] * 5,
        out_specs=[vmem] * 4,
        out_shape=[flat_shape, dense, message_shape, message_shape],
        input_output_aliases={0: 0, 1: 1},
        compiler_params=params,
        name="pack",
    )(own_flat, own_gain, listed, got_p, got_q)
    ring = swaps(lon_total, 1) + [(lon_total - 1, 0), (0, lon_total - 1)]
    got_a = lax.ppermute(to_a, "lon", swaps(lon_total, 0))
    got_b = lax.ppermute(to_b, "lon", ring)

    tile = jax.ShapeDtypeStruct((rows, cols), f32)
    return pl.pallas_call(
        step_kernel,
        in_specs=[smem] + [vmem] * 6,
        out_specs=[vmem] * 4,
        out_shape=[tile] * 4,
        scratch_shapes=[
            pltpu.VMEM((ext + RIM, cols), f32),
            pltpu.VMEM((room, cols), f32),
            pltpu.VMEM((WATER + 1, 2 * total, cols), f32),
            pltpu.VMEM((2, ext + RIM, cols), f32),
            pltpu.VMEM((ext + RIM, cols), f32),
            pltpu.VMEM((2, 2, ext, cols), f32),
            pltpu.VMEM((2, 4, ext, cols), f32),
            pltpu.VMEM((rows + RIM, cols), f32),
            pltpu.VMEM((2, RIM, cols), jnp.int32),
            pltpu.SMEM((cols,), jnp.int32),
            pltpu.SMEM((cols,), jnp.int32),
            pltpu.SemaphoreType.DMA((2,)),
        ],
        compiler_params=params,
        name="steps",
    )(row_list, flat, gain, level, bank_class, got_a, got_b)


def solution(mesh):
    grid = P("lat", "lon")
    return jax.shard_map(
        body,
        mesh=mesh,
        in_specs=(grid,) * 7,
        out_specs=(grid,) * 4,
        check_vma=False,
    )
```

```python
import functools

import jax
import jax.numpy as jnp
from jax import lax
from jax.experimental import pallas as pl
from jax.experimental.pallas import tpu as pltpu
from jax.sharding import PartitionSpec as P

SUB = 8
STEPS = 4

GRAVITY = 9.81
CELL_SIZE = 90.0
TIME_STEP = 10.0
SHALLOW = 0.1
EXCHANGE = 0.01
CHANNEL_MANNING = 0.035

RIM = 8
COLS = SUB * (STEPS - 2)
DURATION = TIME_STEP / SUB
SURFACE, GROUND, ROUGH = range(3)
FLOOD_FIELDS = 3
LEVEL, FLUX, BED, WIDTH, GAIN = range(5)
SLOT_FIELDS = 5
TOP, DRIVE, FRICTION, FEED, WATER = range(5, 10)
ROWS_AT_ONCE = 64
TILES_AT_ONCE = 34
UNPACK_AT_ONCE = 20
FIRST_AT_ONCE = 7


def lanes(shape):
    return lax.broadcasted_iota(jnp.int32, shape, 1)


def sublanes(shape):
    return lax.broadcasted_iota(jnp.int32, shape, 0)


def east_of(field):
    return pltpu.roll(field, field.shape[1] - 1, 1)


def face(flow, here, there, top, drive, friction):
    height = jnp.maximum(here, there) - top
    driven = flow - drive * height * (there - here)
    spread = jnp.exp(jnp.log(height * height + SHALLOW * SHALLOW) * (-7.0 / 6.0))
    resisted = 1.0 + friction * jnp.abs(flow) * spread
    return driven * pl.reciprocal(resisted, approx=True)


def first_face(here, there, top, drive):
    height = jnp.maximum(here, there) - top
    return -(drive * height * (there - here))


def reach_constants(bed, width):
    top = jnp.maximum(bed, east_of(bed))
    breadth = 0.5 * (width + east_of(width))
    inner = lanes(bed.shape) < bed.shape[1] - 1
    drive = jnp.where(inner, (GRAVITY * DURATION / CELL_SIZE) * breadth, 0.0)
    friction = jnp.where(
        inner, (GRAVITY * DURATION * CHANNEL_MANNING * CHANNEL_MANNING) / breadth, 0.0
    )
    feed = (DURATION / CELL_SIZE) / width
    return top, drive, friction, feed


def west_of(field):
    return pltpu.roll(field, 1, 1)


def advanced(level, west, flux, surface, feed):
    transfer = (EXCHANGE * DURATION) * (level - surface)
    return level + ((west - flux) * feed - transfer), transfer


def first_reaches(level, surface, constants):
    top, drive, friction, feed = constants
    west_faces = [west_of(value) for value in (top, drive, friction)]
    flux = first_face(level, east_of(level), top, drive)
    west = first_face(west_of(level), level, west_faces[0], west_faces[1])
    level, gathered = advanced(level, west, flux, surface, feed)

    def substep(_, state):
        level, west, flux, gathered = state
        west = face(west, west_of(level), level, *west_faces)
        flux = face(flux, level, east_of(level), top, drive, friction)
        level, transfer = advanced(level, west, flux, surface, feed)
        return level, west, flux, gathered + transfer

    state = repeated(SUB - 1, FIRST_AT_ONCE, substep, (level, west, flux, gathered))
    return state[0], state[2], state[3]


def odd_position(axis):
    return lax.rem(lax.axis_index(axis), 2)


def repeated(count, unroll, step, carry):
    if unroll >= count:
        for i in range(count):
            carry = step(i, carry)
        return carry

    def some(block, carry):
        for j in range(unroll):
            carry = step(block * unroll + j, carry)
        return carry

    return lax.fori_loop(0, count // unroll, some, carry)


def each_row(count, visit, unroll=ROWS_AT_ONCE):
    repeated(count, unroll, lambda i, carry: (visit(i), carry)[1], 0)


def row_of(tile):
    return tile * RIM if isinstance(tile, int) else pl.multiple_of(tile * RIM, RIM)


def each_tile(count, visit, unroll):
    repeated(count, unroll, lambda i, carry: (visit(row_of(i)), carry)[1], 0)


def rows_kernel(mask_hbm, *refs):
    fields, outs, (reals, classes, mask_ref, sems) = refs[:6], refs[6:8], refs[8:]
    rows = mask_hbm.shape[0]
    northern = odd_position("lat") == 0
    copies = [pltpu.make_async_copy(mask_hbm, mask_ref, sems.at[0])]
    for k, field in enumerate(fields):
        for side, start in enumerate((0, rows - RIM)):
            to = reals.at[side, k] if k < 4 else classes.at[side, k - 4]
            copies.append(
                pltpu.make_async_copy(field.at[pl.ds(start, RIM)], to, sems.at[1 + 2 * k + side])
            )
    for copy in copies:
        copy.start()
    for copy in copies:
        copy.wait()
    shape = reals.shape[2:]
    row = sublanes(shape)

    def rims(side, start):
        depth, ground, rough, river = [reals[side, k] for k in range(4)]
        width, bank = classes[side, 0], classes[side, 1]
        live = jnp.zeros(shape, jnp.float32)
        for j in range(RIM):
            live = jnp.where(row == j, mask_ref[start + j].astype(jnp.float32), live)
        bed = ground - (1.0 + 0.5 * bank.astype(jnp.float32))
        wide = 8.0 + 9.0 * width.astype(jnp.float32)
        return [ground + depth, ground, rough, bed + river, bed, wide, live]

    for k, (low, high) in enumerate(zip(rims(0, 0), rims(1, rows - RIM))):
        outs[0][RIM * k : RIM * (k + 1), :] = jnp.where(northern, high, low)
        outs[1][RIM * k : RIM * (k + 1), :] = jnp.where(northern, low, high)


def fill_list(mask_ref, rows_ref):
    rows = mask_ref.shape[0]
    room = rows // 4
    beyond = rows + 2 * RIM
    batch = 16

    for i in range(room):
        rows_ref[i] = beyond
    count = jnp.int32(0)
    for first in range(0, rows, batch):
        bits = [mask_ref[first + j] for j in range(batch)]
        places = []
        for bit in bits:
            places.append(count)
            count = count + bit
        for j, place in enumerate(places):
            rows_ref[place] = first + j + RIM
    rows_ref[count] = beyond
    return count


def own_kernel(
    mask_any, depth_ref, ground_ref, rough_ref, river_ref, width_ref, bank_ref,
    flat_ref, level_ref, listed_ref,
    bed_ref, wide_ref, mask_ref, rows_ref, sem,
):
    rows, cols = depth_ref.shape
    slots = rows // 4
    tail, ext, total = rows + RIM, rows + 2 * RIM, slots + RIM
    base = FLOOD_FIELDS * ext
    fetch = pltpu.make_async_copy(mask_any, mask_ref, sem)
    fetch.start()

    def prepare(t):
        at = pl.ds(t, RIM)
        ground = ground_ref[at, :]
        bed = ground - (1.0 + 0.5 * bank_ref[at, :].astype(jnp.float32))
        flat_ref[pl.ds(t + (SURFACE * ext + RIM), RIM), :] = ground + depth_ref[at, :]
        flat_ref[pl.ds(t + (GROUND * ext + RIM), RIM), :] = ground
        flat_ref[pl.ds(t + (ROUGH * ext + RIM), RIM), :] = rough_ref[at, :]
        level_ref[at, :] = bed + river_ref[at, :]
        bed_ref[at, :] = bed
        wide_ref[at, :] = 8.0 + 9.0 * width_ref[at, :].astype(jnp.float32)

    each_tile(rows // RIM, prepare, TILES_AT_ONCE)
    zero = jnp.zeros((RIM, cols), jnp.float32)
    flat_ref[SURFACE * ext + tail : (SURFACE + 1) * ext, :] = zero
    level_ref[rows:tail, :] = zero
    bed_ref[rows:tail, :] = zero
    wide_ref[rows:tail, :] = zero + 1.0
    lane = lanes((RIM, cols))
    fetch.wait()
    count = fill_list(mask_ref, rows_ref)

    listed = zero + count.astype(jnp.float32)
    for i in range(slots):
        e = rows_ref[i]
        own = jnp.minimum(e - RIM, rows)
        listed = jnp.where(lane == cols - slots + i, e.astype(jnp.float32), listed)
        to = base + i
        of, surface = pl.ds(own, 1), pl.ds(own + (SURFACE * ext + RIM), 1)
        flat_ref[pl.ds(to + LEVEL * total, 1), :] = level_ref[of, :]
        flat_ref[pl.ds(to + BED * total, 1), :] = bed_ref[of, :]
        flat_ref[pl.ds(to + WIDTH * total, 1), :] = wide_ref[of, :]
        flat_ref[pl.ds(to + GAIN * total, 1), :] = flat_ref[surface, :]
    listed_ref[...] = listed

    def part(field):
        return slice(base + field * total, base + field * total + slots)

    width = flat_ref[part(WIDTH), :]
    level, flux, gathered = first_reaches(
        flat_ref[part(LEVEL), :],
        flat_ref[part(GAIN), :],
        reach_constants(flat_ref[part(BED), :], width),
    )
    flat_ref[part(LEVEL), :] = level
    flat_ref[part(FLUX), :] = flux
    flat_ref[part(GAIN), :] = gathered * (width / CELL_SIZE)


def pack_kernel(rows, own_flat, listed_ref, p_ref, q_ref, flat_ref, a_ref, b_ref):
    del own_flat
    cols = a_ref.shape[1]
    ext = rows + 2 * RIM
    slots = rows // 4
    tail, total = rows + RIM, slots + RIM
    base = FLOOD_FIELDS * ext
    half = RIM // 2
    northern = odd_position("lat") == 0
    p, q = p_ref[...], q_ref[...]
    north = jnp.where(northern, p, q)
    south = jnp.where(northern, q, p)

    def rim(block, k):
        return block[RIM * k : RIM * (k + 1)]

    def ends(k):
        return jnp.concatenate([rim(south, k)[half:], rim(north, k)[:half]], axis=0)

    def part(field):
        start = base + field * total + slots
        return slice(start, start + RIM)

    bed, width = ends(4), ends(5)
    level, flux, gathered = first_reaches(ends(3), ends(0), reach_constants(bed, width))
    gained = jnp.where(ends(6) > 0.0, gathered * (width / CELL_SIZE), 0.0)
    for field, value in (
        (LEVEL, level), (FLUX, flux), (BED, bed), (WIDTH, width), (GAIN, gained),
    ):
        flat_ref[part(field), :] = value
    live = base + SLOT_FIELDS * total
    flat_ref[live : live + RIM, :] = ends(6)
    for k in range(FLOOD_FIELDS):
        flat_ref[k * ext : k * ext + RIM, :] = rim(south, k)
        flat_ref[k * ext + tail : (k + 1) * ext, :] = rim(north, k)

    groups = cols // COLS
    group = lanes((RIM, cols)) // COLS
    eastern = odd_position("lon") == 0
    tiles = (base + SLOT_FIELDS * total) // RIM + 1
    turns = []
    for start in (jnp.where(eastern, cols - COLS, 0), jnp.where(eastern, 0, cols - COLS)):
        turns.append([lax.rem(cols + COLS * g - start, cols) for g in range(groups)])

    def pack(m, used):
        block_a = block_b = listed_ref[...]
        for g in range(used):
            source = flat_ref[pl.ds(row_of(m * groups + g), RIM), :]
            block_a = jnp.where(group == g, pltpu.roll(source, turns[0][g], 1), block_a)
            block_b = jnp.where(group == g, pltpu.roll(source, turns[1][g], 1), block_b)
        to = pl.ds(row_of(m), RIM)
        a_ref[to, :] = block_a
        b_ref[to, :] = block_b

    each_row(tiles // groups, lambda m: pack(m, groups), UNPACK_AT_ONCE)
    pack(tiles // groups, tiles % groups)


def step_kernel(
    flat_ref, level_ref, bank_ref, listed_ref, a_ref, b_ref,
    depth_out, river_out, east_out, north_out,
    both_ref, state, gains,
    flow_ref, fixed_ref, river_ref, list_rows, list_smem, sems,
):
    rows, cols = depth_out.shape
    slots = rows // 4
    tail, ext, total = rows + RIM, rows + 2 * RIM, slots + RIM
    base = FLOOD_FIELDS * ext
    half = RIM // 2
    lat_number, lat_total = lax.axis_index("lat"), lax.axis_size("lat")
    eastern = odd_position("lon") == 0
    lists = a_ref.shape[0] - RIM
    zero = jnp.zeros((RIM, cols), jnp.float32)

    few = slots // 4
    apart = ext + RIM
    own_ref = both_ref.at[pl.ds(0, apart), :]
    side_ref = both_ref.at[pl.ds(apart, both_ref.shape[0] - apart), :]

    own_list = listed_ref[...]
    crowded = jnp.broadcast_to(own_list[:, 0:1], own_list.shape) > few + 0.5
    list_a, list_b = a_ref[lists : lists + RIM, :], b_ref[lists : lists + RIM, :]
    east_list = jnp.where(eastern, list_a, list_b) + apart
    west_list = jnp.where(eastern, list_b, list_a) + apart
    copies = []
    for k, rows_of in enumerate((
        jnp.where(crowded, own_list, east_list), jnp.where(crowded, own_list, west_list),
        jnp.where(crowded, east_list, own_list), jnp.where(crowded, west_list, own_list),
        own_list,
    )):
        list_rows[k] = rows_of.astype(jnp.int32)
        copies.append(pltpu.make_async_copy(list_rows.at[k, 0], list_smem.at[k], sems.at[k]))
        copies[k].start()

    groups = cols // COLS
    lane = lanes((RIM, cols))
    low = lane < cols // 2
    use_a = low == eastern
    turns = []
    for to in (jnp.where(eastern, 0, cols - COLS), jnp.where(eastern, cols - COLS, 0)):
        turns.append([lax.rem(cols + to - COLS * g, cols) for g in range(groups)])

    def unpack(m):
        at = pl.ds(row_of(m), RIM)
        block_a, block_b = a_ref[at, :], b_ref[at, :]
        for g in range(groups):
            from_a = pltpu.roll(block_a, turns[0][g], 1)
            from_b = pltpu.roll(block_b, turns[1][g], 1)
            to = pl.ds(row_of(m * groups + g), RIM)
            side_ref[to, :] = jnp.where(use_a, from_a, from_b)

    each_row(a_ref.shape[0] // RIM, unpack, UNPACK_AT_ONCE)

    def copy_in(t):
        at, beside = pl.ds(t, RIM), pl.ds(apart + t, RIM)
        own_ref[at, :] = flat_ref[at, :]
        for k in range(2):
            gains[k, at, :] = zero
            gains[k, beside, :] = zero

    each_tile(ext // RIM, copy_in, TILES_AT_ONCE)
    own_ref[ext : ext + RIM, :] = zero

    def chosen(own, side):
        return jnp.where(crowded, own, side), jnp.where(crowded, side, own)

    for t in range(0, total, RIM):
        pairs = []
        for field in range(SLOT_FIELDS):
            at = pl.ds(base + field * total + t, RIM)
            pairs.append(chosen(flat_ref[at, :], side_ref[at, :]))
        for j in range(2):
            to = t
            if j == 1:
                if few <= t < slots:
                    continue
                to = total + min(t, few)
            constants = reach_constants(pairs[BED][j], pairs[WIDTH][j])
            for field, pair in enumerate(pairs):
                state[field, to : to + RIM, :] = pair[j]
            for field, value in zip((TOP, DRIVE, FRICTION, FEED), constants):
                state[field, to : to + RIM, :] = value
    at = pl.ds(base + SLOT_FIELDS * total, RIM)
    alive = [value > 0.0 for value in chosen(flat_ref[at, :], side_ref[at, :])]
    for copy in copies:
        copy.wait()
    first = cols - slots
    places = [(i, list_smem.at[0], list_smem.at[1], first + i) for i in range(slots)]
    places += [(total + i, list_smem.at[2], list_smem.at[3], first + i) for i in range(few)]
    edge = total + few

    def spread():
        for slot, lows, highs, i in places:
            line = state[GAIN, slot : slot + 1, :]
            gains[0, pl.ds(lows[i], 1), :] = line
            gains[1, pl.ds(highs[i], 1), :] = line
        for j, lines in enumerate(
            chosen(state[GAIN, slots:total, :], state[GAIN, edge : edge + RIM, :])
        ):
            for k in range(2):
                start = j * apart
                gains[k, start + half : start + RIM, :] = lines[:half]
                gains[k, start + tail : start + tail + half, :] = lines[half:]

    middle = lanes((1, cols)) < cols // 2

    def draw():
        for slot, lows, highs, i in places:
            state[WATER, slot : slot + 1, :] = jnp.where(
                middle, both_ref[pl.ds(lows[i], 1), :], both_ref[pl.ds(highs[i], 1), :]
            )
        ends = [
            jnp.concatenate([ref[half:RIM, :], ref[tail : tail + half, :]], axis=0)
            for ref in (own_ref, side_ref)
        ]
        for start, value in zip((slots, edge), chosen(*ends)):
            state[WATER, start : start + RIM, :] = value

    spread()

    def reaches(start, size, live):
        at = slice(start, start + size)

        faces = [state[k, at, :] for k in (TOP, DRIVE, FRICTION)]
        west_faces = [west_of(value) for value in faces]
        surface, feed = state[WATER, at, :], state[FEED, at, :]

        level, flux = state[LEVEL, at, :], state[FLUX, at, :]
        west, gathered = west_of(flux), jnp.zeros_like(level)
        for _ in range(SUB):
            west = face(west, west_of(level), level, *west_faces)
            flux = face(flux, level, east_of(level), *faces)
            level, transfer = advanced(level, west, flux, surface, feed)
            gathered = gathered + transfer
            yield
        state[LEVEL, at, :] = level
        state[FLUX, at, :] = flux
        gained = gathered * (state[WIDTH, at, :] / CELL_SIZE)
        fixed = size - RIM
        state[GAIN, start : start + fixed, :] = gained[:fixed]
        state[GAIN, start + fixed : start + size, :] = jnp.where(live, gained[fixed:], 0.0)

    last_lane = lane == cols - 1
    first_lane = lane == 0
    row = sublanes((RIM, cols))
    first_row = row == 0
    drive = GRAVITY * TIME_STEP / CELL_SIZE
    share = TIME_STEP / CELL_SIZE
    edge_south = jnp.where(lat_number == 0, RIM - 1, -1)
    edge_north = jnp.where(lat_number == lat_total - 1, tail - 1, -1)

    def pair_east(own, side):
        a, b = east_of(own), east_of(side)
        return jnp.where(last_lane, b, a), jnp.where(last_lane, a, b)

    def pair_west(own, side):
        a, b = pltpu.roll(own, 1, 1), pltpu.roll(side, 1, 1)
        return jnp.where(first_lane, b, a), jnp.where(first_lane, a, b)

    def constants_of(t):
        at = pl.ds(t, RIM)

        def read(field, shift):
            where = pl.ds(t + (field * ext + shift), RIM)
            return flat_ref[where, :], side_ref[where, :]

        ground, rough = read(GROUND, 0), read(ROUGH, 0)
        ground_north, rough_north = read(GROUND, 1), read(ROUGH, 1)
        ground_east, rough_east = pair_east(*ground), pair_east(*rough)
        weight = GRAVITY * TIME_STEP
        for j in range(2):
            fixed_ref[j, 0, at, :] = jnp.maximum(ground[j], ground_east[j])
            fixed_ref[j, 1, at, :] = weight * (rough[j] * rough_east[j])
            fixed_ref[j, 2, at, :] = jnp.maximum(ground[j], ground_north[j])
            fixed_ref[j, 3, at, :] = weight * (rough[j] * rough_north[j])

    def north_flow(j, t, here, step):
        at = pl.ds(t, RIM)
        north = (own_ref, side_ref)[j][pl.ds(t + 1, RIM), :]
        top = fixed_ref[j, 2, at, :]
        if step == 0:
            flow = first_face(here, north, top, drive)
        else:
            flow = face(flow_ref[j, 1, at, :], here, north, top, drive, fixed_ref[j, 3, at, :])
        e = t + row
        return jnp.where((e == edge_south) | (e == edge_north), 0.0, flow)

    def flows(t, step):
        at = pl.ds(t, RIM)
        final = step == STEPS - 1
        here = own_ref[at, :], side_ref[at, :]
        for j in range(1 if final else 2):
            flow_ref[j, 1, at, :] = north_flow(j, t, here[j], step)
        if final and t == 0:
            return
        east = pair_east(*here)
        for j in range(2):
            top = fixed_ref[j, 0, at, :]
            if step == 0:
                flow = first_face(here[j], east[j], top, drive)
            else:
                flow = face(
                    flow_ref[j, 0, at, :], here[j], east[j], top, drive, fixed_ref[j, 1, at, :]
                )
            flow_ref[j, 0, at, :] = flow

    def update(t, before, step):
        at = pl.ds(t, RIM)
        final = step == STEPS - 1
        to_east = flow_ref[0, 0, at, :], flow_ref[1, 0, at, :]
        west = pair_west(*to_east)
        after = []
        for j in range(1 if final else 2):
            to_north = flow_ref[j, 1, at, :]
            turned = pltpu.roll(to_north, 1, 0)
            south = jnp.where(first_row, before[j], turned)
            after.append(turned)
            moved = share * (west[j] - to_east[j] + south - to_north)
            if final:
                out = pl.ds(t - RIM, RIM)
                new = own_ref[at, :] + moved + gains[0, at, :]
                depth_out[out, :] = new - flat_ref[pl.ds(t + GROUND * ext, RIM), :]
                east_out[out, :] = to_east[0]
                north_out[out, :] = to_north
            elif j == 0:
                own_ref[at, :] = own_ref[at, :] + moved + gains[0, at, :]
            else:
                beside = pl.ds(apart + t, RIM)
                gain = jnp.where(low, gains[0, beside, :], gains[1, beside, :])
                side_ref[at, :] = side_ref[at, :] + moved + gain
        return after

    def update_all(step):
        if step == STEPS - 1:
            before = (pltpu.roll(flow_ref[0, 1, 0:RIM, :], 1, 0),)
            tiles = range(RIM, tail, RIM)
        else:
            before = (zero, zero)
            tiles = range(0, ext, RIM)
        for t in tiles:
            before = update(t, before, step)

    def settle():
        river_ref[0:rows, :] = level_ref[0:rows, :]
        for i in range(slots):
            own = jnp.minimum(list_smem[4, first + i] - RIM, rows)
            other = total + min(i, few)
            river_ref[pl.ds(own, 1), :] = jnp.where(
                crowded[:1], state[LEVEL, i : i + 1, :], state[LEVEL, other : other + 1, :]
            )
        for t in range(0, rows, RIM):
            at = pl.ds(t, RIM)
            ground = flat_ref[pl.ds(t + (GROUND * ext + RIM), RIM), :]
            bed = ground - (1.0 + 0.5 * bank_ref[at, :].astype(jnp.float32))
            river_out[at, :] = river_ref[at, :] - bed

    for t in range(0, ext, RIM):
        constants_of(t)
        flows(t, 0)
    update_all(0)
    for step in range(1, STEPS):
        final = step == STEPS - 1
        draw()

        running = [reaches(0, total, alive[0]), reaches(total, few + RIM, alive[1])]
        tiles = list(range(0, tail if final else ext, RIM))
        share_of = -(-len(tiles) // SUB)
        for substep in range(SUB):
            for reach in running:
                next(reach)
            for t in tiles[substep * share_of : (substep + 1) * share_of]:
                flows(t, step)
        for reach in running:
            next(reach, None)
        spread()
        if final:
            settle()
        update_all(step)


def swaps(count, first):
    pairs = [(i, i + 1) for i in range(first, count - 1, 2)]
    return pairs + [(b, a) for a, b in pairs]


def body(depth_init, ground, roughness, river_init, reach_mask, width_class, bank_class):
    rows, cols = ground.shape
    slots = rows // 4
    f32 = jnp.float32
    lon_total, lat_total = lax.axis_size("lon"), lax.axis_size("lat")
    mask = reach_mask.reshape(rows)
    vmem = pl.BlockSpec(memory_space=pltpu.VMEM)
    fields = (depth_init, ground, roughness, river_init, width_class, bank_class)
    ext, total = rows + 2 * RIM, slots + RIM
    used = FLOOD_FIELDS * ext + SLOT_FIELDS * total + RIM
    groups = cols // COLS
    message = -(-(used // RIM + slots // COLS) // groups) * RIM
    room = message * groups
    params = pltpu.CompilerParams(vmem_limit_bytes=48 * 1024 * 1024)

    hbm = pl.BlockSpec(memory_space=pltpu.HBM)
    rim_shape = jax.ShapeDtypeStruct((7 * RIM, cols), f32)
    to_p, to_q = pl.pallas_call(
        rows_kernel,
        in_specs=[hbm] * 7,
        out_specs=[vmem, vmem],
        out_shape=[rim_shape, rim_shape],
        scratch_shapes=[
            pltpu.VMEM((2, 4, RIM, cols), f32),
            pltpu.VMEM((2, 2, RIM, cols), jnp.int32),
            pltpu.SMEM((rows,), jnp.int32),
            pltpu.SemaphoreType.DMA((13,)),
        ],
        compiler_params=pltpu.CompilerParams(vmem_limit_bytes=63 * 1024 * 1024),
        name="rims",
    )(mask, *fields)
    got_p = lax.ppermute(to_p, "lat", swaps(lat_total, 0))
    got_q = lax.ppermute(to_q, "lat", swaps(lat_total, 1))
    flat_shape = jax.ShapeDtypeStruct((room, cols), f32)
    own_flat, level, listed = pl.pallas_call(
        own_kernel,
        in_specs=[pl.BlockSpec(memory_space=pl.ANY)] + [vmem] * 6,
        out_specs=[vmem] * 3,
        out_shape=[
            flat_shape,
            jax.ShapeDtypeStruct((rows + RIM, cols), f32),
            jax.ShapeDtypeStruct((RIM, cols), f32),
        ],
        scratch_shapes=[pltpu.VMEM((rows + RIM, cols), f32)] * 2
        + [
            pltpu.SMEM((rows,), jnp.int32),
            pltpu.SMEM((2 * slots,), jnp.int32),
            pltpu.SemaphoreType.DMA,
        ],
        compiler_params=params,
        name="own_reaches",
    )(mask, *fields)

    message_shape = jax.ShapeDtypeStruct((message, cols), f32)
    flat, to_a, to_b = pl.pallas_call(
        functools.partial(pack_kernel, rows),
        in_specs=[vmem] * 4,
        out_specs=[vmem] * 3,
        out_shape=[flat_shape, message_shape, message_shape],
        input_output_aliases={0: 0},
        compiler_params=params,
        name="pack",
    )(own_flat, listed, got_p, got_q)
    ring = swaps(lon_total, 1) + [(lon_total - 1, 0), (0, lon_total - 1)]
    got_a = lax.ppermute(to_a, "lon", swaps(lon_total, 0))
    got_b = lax.ppermute(to_b, "lon", ring)

    tile = jax.ShapeDtypeStruct((rows, cols), f32)
    return pl.pallas_call(
        step_kernel,
        in_specs=[vmem] * 6,
        out_specs=[vmem] * 4,
        out_shape=[tile] * 4,
        scratch_shapes=[
            pltpu.VMEM((ext + RIM + room, cols), f32),
            pltpu.VMEM((WATER + 1, total + slots // 4 + RIM, cols), f32),
            pltpu.VMEM((2, 2 * (ext + RIM), cols), f32),
            pltpu.VMEM((2, 2, ext, cols), f32),
            pltpu.VMEM((2, 4, ext, cols), f32),
            pltpu.VMEM((rows + RIM, cols), f32),
            pltpu.VMEM((5, RIM, cols), jnp.int32),
            pltpu.SMEM((5, cols), jnp.int32),
            pltpu.SemaphoreType.DMA((5,)),
        ],
        compiler_params=params,
        name="steps",
    )(flat, level, bank_class, listed, got_a, got_b)


def solution(mesh):
    grid = P("lat", "lon")
    return jax.shard_map(
        body,
        mesh=mesh,
        in_specs=(grid,) * 7,
        out_specs=(grid,) * 4,
        check_vma=False,
    )
```

```python
import functools

import jax
import jax.numpy as jnp
from jax import lax
from jax.experimental import pallas as pl
from jax.experimental.pallas import tpu as pltpu
from jax.sharding import PartitionSpec as P

SUB = 8
STEPS = 4

GRAVITY = 9.81
CELL_SIZE = 90.0
TIME_STEP = 10.0
SHALLOW = 0.1
EXCHANGE = 0.01
CHANNEL_MANNING = 0.035

RIM = 8
COLS = SUB * (STEPS - 2)
DURATION = TIME_STEP / SUB
SURFACE, GROUND, ROUGH = range(3)
FLOOD_FIELDS = 3
LEVEL, FLUX, BED, WIDTH, GAIN = range(5)
SLOT_FIELDS = 5
TOP, DRIVE, FRICTION, FEED, WATER = range(5, 10)
ROWS_AT_ONCE = 64
TILES_AT_ONCE = 34
UNPACK_AT_ONCE = 20


def lanes(shape):
    return lax.broadcasted_iota(jnp.int32, shape, 1)


def sublanes(shape):
    return lax.broadcasted_iota(jnp.int32, shape, 0)


def east_of(field):
    return pltpu.roll(field, field.shape[1] - 1, 1)


def face(flow, here, there, top, drive, friction):
    height = jnp.maximum(here, there) - top
    driven = flow - drive * height * (there - here)
    spread = jnp.exp(jnp.log(height * height + SHALLOW * SHALLOW) * (-7.0 / 6.0))
    resisted = 1.0 + friction * jnp.abs(flow) * spread
    return driven * pl.reciprocal(resisted, approx=True)


def first_face(here, there, top, drive):
    height = jnp.maximum(here, there) - top
    return -(drive * height * (there - here))


def reach_constants(bed, width):
    top = jnp.maximum(bed, east_of(bed))
    breadth = 0.5 * (width + east_of(width))
    inner = lanes(bed.shape) < bed.shape[1] - 1
    drive = jnp.where(inner, (GRAVITY * DURATION / CELL_SIZE) * breadth, 0.0)
    friction = jnp.where(
        inner, (GRAVITY * DURATION * CHANNEL_MANNING * CHANNEL_MANNING) / breadth, 0.0
    )
    feed = (DURATION / CELL_SIZE) / width
    return top, drive, friction, feed


def west_of(field):
    return pltpu.roll(field, 1, 1)


def advanced(level, west, flux, surface, feed):
    transfer = (EXCHANGE * DURATION) * (level - surface)
    return level + ((west - flux) * feed - transfer), transfer


def first_reaches(level, surface, constants):
    feed = constants[3]
    faces = constants[:3]
    far_east = [east_of(value) for value in faces]
    near_west = [west_of(value) for value in faces]
    far_west = [west_of(value) for value in near_west]
    feeds = west_of(feed), feed, east_of(feed)
    waters = west_of(surface), surface, east_of(surface)
    west = flux = gathered = None
    for pair in range(SUB // 2):
        levels = [west_of(level), level, east_of(level)]
        around = [pltpu.roll(level, 2, 1)] + levels + [pltpu.roll(level, level.shape[1] - 2, 1)]
        if pair:
            flows = [west_of(west), west, flux, east_of(flux)]
        else:
            flows = [None] * 4
        sets = [far_west, near_west, faces, far_east]
        for k in range(4):
            if pair:
                flows[k] = face(flows[k], around[k], around[k + 1], *sets[k])
            else:
                flows[k] = first_face(around[k], around[k + 1], *sets[k][:2])
        for k in range(3):
            levels[k], transfer = advanced(levels[k], flows[k], flows[k + 1], waters[k], feeds[k])
            if k == 1:
                gathered = transfer if gathered is None else gathered + transfer
        west = face(flows[1], levels[0], levels[1], *near_west)
        flux = face(flows[2], levels[1], levels[2], *faces)
        level, transfer = advanced(levels[1], west, flux, surface, feed)
        gathered = gathered + transfer
    return level, flux, gathered


def odd_position(axis):
    return lax.rem(lax.axis_index(axis), 2)


def repeated(count, unroll, step, carry):
    if unroll >= count:
        for i in range(count):
            carry = step(i, carry)
        return carry

    def some(block, carry):
        for j in range(unroll):
            carry = step(block * unroll + j, carry)
        return carry

    return lax.fori_loop(0, count // unroll, some, carry)


def each_row(count, visit, unroll=ROWS_AT_ONCE):
    repeated(count, unroll, lambda i, carry: (visit(i), carry)[1], 0)


def row_of(tile):
    return tile * RIM if isinstance(tile, int) else pl.multiple_of(tile * RIM, RIM)


def each_tile(count, visit, unroll):
    repeated(count, unroll, lambda i, carry: (visit(row_of(i)), carry)[1], 0)


def rows_kernel(mask_hbm, *refs):
    fields, outs, (reals, classes, mask_ref, sems) = refs[:6], refs[6:8], refs[8:]
    rows = mask_hbm.shape[0]
    northern = odd_position("lat") == 0
    copies = [pltpu.make_async_copy(mask_hbm, mask_ref, sems.at[0])]
    for k, field in enumerate(fields):
        for side, start in enumerate((0, rows - RIM)):
            to = reals.at[side, k] if k < 4 else classes.at[side, k - 4]
            copies.append(
                pltpu.make_async_copy(field.at[pl.ds(start, RIM)], to, sems.at[1 + 2 * k + side])
            )
    for copy in copies:
        copy.start()
    for copy in copies:
        copy.wait()
    shape = reals.shape[2:]
    row = sublanes(shape)

    def rims(side, start):
        depth, ground, rough, river = [reals[side, k] for k in range(4)]
        width, bank = classes[side, 0], classes[side, 1]
        live = jnp.zeros(shape, jnp.float32)
        for j in range(RIM):
            live = jnp.where(row == j, mask_ref[start + j].astype(jnp.float32), live)
        bed = ground - (1.0 + 0.5 * bank.astype(jnp.float32))
        wide = 8.0 + 9.0 * width.astype(jnp.float32)
        return [ground + depth, ground, rough, bed + river, bed, wide, live]

    for k, (low, high) in enumerate(zip(rims(0, 0), rims(1, rows - RIM))):
        outs[0][RIM * k : RIM * (k + 1), :] = jnp.where(northern, high, low)
        outs[1][RIM * k : RIM * (k + 1), :] = jnp.where(northern, low, high)


def fill_list(mask_ref, rows_ref):
    rows = mask_ref.shape[0]
    room = rows // 4
    beyond = rows + 2 * RIM
    batch = 16

    for i in range(room):
        rows_ref[i] = beyond
    count = jnp.int32(0)
    for first in range(0, rows, batch):
        bits = [mask_ref[first + j] for j in range(batch)]
        places = []
        for bit in bits:
            places.append(count)
            count = count + bit
        for j, place in enumerate(places):
            rows_ref[place] = first + j + RIM
    rows_ref[count] = beyond
    return count


def own_kernel(
    mask_any, depth_ref, ground_ref, rough_ref, river_ref, width_ref, bank_ref,
    flat_ref, level_ref, listed_ref,
    bed_ref, wide_ref, mask_ref, rows_ref, sem,
):
    rows, cols = depth_ref.shape
    slots = rows // 4
    tail, ext, total = rows + RIM, rows + 2 * RIM, slots + RIM
    base = FLOOD_FIELDS * ext
    fetch = pltpu.make_async_copy(mask_any, mask_ref, sem)
    fetch.start()

    def prepare(t):
        at = pl.ds(t, RIM)
        ground = ground_ref[at, :]
        bed = ground - (1.0 + 0.5 * bank_ref[at, :].astype(jnp.float32))
        flat_ref[pl.ds(t + (SURFACE * ext + RIM), RIM), :] = ground + depth_ref[at, :]
        flat_ref[pl.ds(t + (GROUND * ext + RIM), RIM), :] = ground
        flat_ref[pl.ds(t + (ROUGH * ext + RIM), RIM), :] = rough_ref[at, :]
        level_ref[at, :] = bed + river_ref[at, :]
        bed_ref[at, :] = bed
        wide_ref[at, :] = 8.0 + 9.0 * width_ref[at, :].astype(jnp.float32)

    each_tile(rows // RIM, prepare, TILES_AT_ONCE)
    zero = jnp.zeros((RIM, cols), jnp.float32)
    flat_ref[SURFACE * ext + tail : (SURFACE + 1) * ext, :] = zero
    level_ref[rows:tail, :] = zero
    bed_ref[rows:tail, :] = zero
    wide_ref[rows:tail, :] = zero + 1.0
    lane = lanes((RIM, cols))
    fetch.wait()
    count = fill_list(mask_ref, rows_ref)

    listed = zero + count.astype(jnp.float32)
    for i in range(slots):
        e = rows_ref[i]
        own = jnp.minimum(e - RIM, rows)
        listed = jnp.where(lane == cols - slots + i, e.astype(jnp.float32), listed)
        to = base + i
        of, surface = pl.ds(own, 1), pl.ds(own + (SURFACE * ext + RIM), 1)
        flat_ref[pl.ds(to + LEVEL * total, 1), :] = level_ref[of, :]
        flat_ref[pl.ds(to + BED * total, 1), :] = bed_ref[of, :]
        flat_ref[pl.ds(to + WIDTH * total, 1), :] = wide_ref[of, :]
        flat_ref[pl.ds(to + GAIN * total, 1), :] = flat_ref[surface, :]
    listed_ref[...] = listed

    def part(field):
        return slice(base + field * total, base + field * total + slots)

    width = flat_ref[part(WIDTH), :]
    level, flux, gathered = first_reaches(
        flat_ref[part(LEVEL), :],
        flat_ref[part(GAIN), :],
        reach_constants(flat_ref[part(BED), :], width),
    )
    flat_ref[part(LEVEL), :] = level
    flat_ref[part(FLUX), :] = flux
    flat_ref[part(GAIN), :] = gathered * (width / CELL_SIZE)


def pack_kernel(rows, own_flat, listed_ref, p_ref, q_ref, flat_ref, a_ref, b_ref):
    del own_flat
    cols = a_ref.shape[1]
    ext = rows + 2 * RIM
    slots = rows // 4
    tail, total = rows + RIM, slots + RIM
    base = FLOOD_FIELDS * ext
    half = RIM // 2
    northern = odd_position("lat") == 0
    p, q = p_ref[...], q_ref[...]
    north = jnp.where(northern, p, q)
    south = jnp.where(northern, q, p)

    def rim(block, k):
        return block[RIM * k : RIM * (k + 1)]

    def ends(k):
        return jnp.concatenate([rim(south, k)[half:], rim(north, k)[:half]], axis=0)

    def part(field):
        start = base + field * total + slots
        return slice(start, start + RIM)

    bed, width = ends(4), ends(5)
    level, flux, gathered = first_reaches(ends(3), ends(0), reach_constants(bed, width))
    gained = jnp.where(ends(6) > 0.0, gathered * (width / CELL_SIZE), 0.0)
    for field, value in (
        (LEVEL, level), (FLUX, flux), (BED, bed), (WIDTH, width), (GAIN, gained),
    ):
        flat_ref[part(field), :] = value
    live = base + SLOT_FIELDS * total
    flat_ref[live : live + RIM, :] = ends(6)
    for k in range(FLOOD_FIELDS):
        flat_ref[k * ext : k * ext + RIM, :] = rim(south, k)
        flat_ref[k * ext + tail : (k + 1) * ext, :] = rim(north, k)

    groups = cols // COLS
    group = lanes((RIM, cols)) // COLS
    eastern = odd_position("lon") == 0
    tiles = (base + SLOT_FIELDS * total) // RIM + 1
    turns = []
    for start in (jnp.where(eastern, cols - COLS, 0), jnp.where(eastern, 0, cols - COLS)):
        turns.append([lax.rem(cols + COLS * g - start, cols) for g in range(groups)])

    def pack(m, used):
        block_a = block_b = listed_ref[...]
        for g in range(used):
            source = flat_ref[pl.ds(row_of(m * groups + g), RIM), :]
            block_a = jnp.where(group == g, pltpu.roll(source, turns[0][g], 1), block_a)
            block_b = jnp.where(group == g, pltpu.roll(source, turns[1][g], 1), block_b)
        to = pl.ds(row_of(m), RIM)
        a_ref[to, :] = block_a
        b_ref[to, :] = block_b

    each_row(tiles // groups, lambda m: pack(m, groups), UNPACK_AT_ONCE)
    pack(tiles // groups, tiles % groups)


def step_kernel(
    flat_ref, level_ref, bank_ref, listed_ref, a_ref, b_ref,
    depth_out, river_out, east_out, north_out,
    both_ref, state, gains,
    flow_ref, fixed_ref, river_ref, list_rows, list_smem, depth_ref, sems, out_sems,
):
    rows, cols = depth_out.shape
    slots = rows // 4
    tail, ext, total = rows + RIM, rows + 2 * RIM, slots + RIM
    base = FLOOD_FIELDS * ext
    half = RIM // 2
    lat_number, lat_total = lax.axis_index("lat"), lax.axis_size("lat")
    eastern = odd_position("lon") == 0
    lists = a_ref.shape[0] - RIM
    zero = jnp.zeros((RIM, cols), jnp.float32)

    few = slots // 4
    apart = ext + RIM
    own_ref = both_ref.at[pl.ds(0, apart), :]
    side_ref = both_ref.at[pl.ds(apart, both_ref.shape[0] - apart), :]

    own_list = listed_ref[...]
    crowded = jnp.broadcast_to(own_list[:, 0:1], own_list.shape) > few + 0.5
    list_a, list_b = a_ref[lists : lists + RIM, :], b_ref[lists : lists + RIM, :]
    east_list = jnp.where(eastern, list_a, list_b) + apart
    west_list = jnp.where(eastern, list_b, list_a) + apart
    copies = []
    for k, rows_of in enumerate((
        jnp.where(crowded, own_list, east_list), jnp.where(crowded, own_list, west_list),
        jnp.where(crowded, east_list, own_list), jnp.where(crowded, west_list, own_list),
        own_list,
    )):
        list_rows[k] = rows_of.astype(jnp.int32)
        copies.append(pltpu.make_async_copy(list_rows.at[k, 0], list_smem.at[k], sems.at[k]))
        copies[k].start()

    groups = cols // COLS
    lane = lanes((RIM, cols))
    low = lane < cols // 2
    use_a = low == eastern
    turns = []
    for to in (jnp.where(eastern, 0, cols - COLS), jnp.where(eastern, cols - COLS, 0)):
        turns.append([lax.rem(cols + to - COLS * g, cols) for g in range(groups)])

    def unpack(m):
        at = pl.ds(row_of(m), RIM)
        block_a, block_b = a_ref[at, :], b_ref[at, :]
        for g in range(groups):
            from_a = pltpu.roll(block_a, turns[0][g], 1)
            from_b = pltpu.roll(block_b, turns[1][g], 1)
            to = pl.ds(row_of(m * groups + g), RIM)
            side_ref[to, :] = jnp.where(use_a, from_a, from_b)

    each_row(a_ref.shape[0] // RIM, unpack, UNPACK_AT_ONCE)

    def copy_in(t):
        at, beside = pl.ds(t, RIM), pl.ds(apart + t, RIM)
        own_ref[at, :] = flat_ref[at, :]
        for k in range(2):
            gains[k, at, :] = zero
            gains[k, beside, :] = zero

    each_tile(ext // RIM, copy_in, TILES_AT_ONCE)
    own_ref[ext : ext + RIM, :] = zero

    def chosen(own, side):
        return jnp.where(crowded, own, side), jnp.where(crowded, side, own)

    for t in range(0, total, RIM):
        pairs = []
        for field in range(SLOT_FIELDS):
            at = pl.ds(base + field * total + t, RIM)
            pairs.append(chosen(flat_ref[at, :], side_ref[at, :]))
        for j in range(2):
            to = t
            if j == 1:
                if few <= t < slots:
                    continue
                to = total + min(t, few)
            constants = reach_constants(pairs[BED][j], pairs[WIDTH][j])
            for field, pair in enumerate(pairs):
                state[field, to : to + RIM, :] = pair[j]
            for field, value in zip((TOP, DRIVE, FRICTION, FEED), constants):
                state[field, to : to + RIM, :] = value
    at = pl.ds(base + SLOT_FIELDS * total, RIM)
    alive = [value > 0.0 for value in chosen(flat_ref[at, :], side_ref[at, :])]
    for copy in copies:
        copy.wait()
    first = cols - slots
    places = [(i, list_smem.at[0], list_smem.at[1], first + i) for i in range(slots)]
    places += [(total + i, list_smem.at[2], list_smem.at[3], first + i) for i in range(few)]
    edge = total + few

    def spread():
        for slot, lows, highs, i in places:
            line = state[GAIN, slot : slot + 1, :]
            gains[0, pl.ds(lows[i], 1), :] = line
            gains[1, pl.ds(highs[i], 1), :] = line
        for j, lines in enumerate(
            chosen(state[GAIN, slots:total, :], state[GAIN, edge : edge + RIM, :])
        ):
            for k in range(2):
                start = j * apart
                gains[k, start + half : start + RIM, :] = lines[:half]
                gains[k, start + tail : start + tail + half, :] = lines[half:]

    middle = lanes((1, cols)) < cols // 2

    def draw():
        for slot, lows, highs, i in places:
            state[WATER, slot : slot + 1, :] = jnp.where(
                middle, both_ref[pl.ds(lows[i], 1), :], both_ref[pl.ds(highs[i], 1), :]
            )
        ends = [
            jnp.concatenate([ref[half:RIM, :], ref[tail : tail + half, :]], axis=0)
            for ref in (own_ref, side_ref)
        ]
        for start, value in zip((slots, edge), chosen(*ends)):
            state[WATER, start : start + RIM, :] = value

    spread()

    def reaches(start, size, live):
        at = slice(start, start + size)

        faces = [state[k, at, :] for k in (TOP, DRIVE, FRICTION)]
        west_faces = [west_of(value) for value in faces]
        surface, feed = state[WATER, at, :], state[FEED, at, :]

        level, flux = state[LEVEL, at, :], state[FLUX, at, :]
        west, gathered = west_of(flux), jnp.zeros_like(level)
        for _ in range(SUB):
            west = face(west, west_of(level), level, *west_faces)
            flux = face(flux, level, east_of(level), *faces)
            level, transfer = advanced(level, west, flux, surface, feed)
            gathered = gathered + transfer
            yield
        state[LEVEL, at, :] = level
        state[FLUX, at, :] = flux
        gained = gathered * (state[WIDTH, at, :] / CELL_SIZE)
        fixed = size - RIM
        state[GAIN, start : start + fixed, :] = gained[:fixed]
        state[GAIN, start + fixed : start + size, :] = jnp.where(live, gained[fixed:], 0.0)

    last_lane = lane == cols - 1
    first_lane = lane == 0
    row = sublanes((RIM, cols))
    first_row = row == 0
    drive = GRAVITY * TIME_STEP / CELL_SIZE
    share = TIME_STEP / CELL_SIZE
    edge_south = jnp.where(lat_number == 0, RIM - 1, -1)
    edge_north = jnp.where(lat_number == lat_total - 1, tail - 1, -1)

    def pair_east(own, side):
        a, b = east_of(own), east_of(side)
        return jnp.where(last_lane, b, a), jnp.where(last_lane, a, b)

    def pair_west(own, side):
        a, b = pltpu.roll(own, 1, 1), pltpu.roll(side, 1, 1)
        return jnp.where(first_lane, b, a), jnp.where(first_lane, a, b)

    def constants_of(t):
        at = pl.ds(t, RIM)

        def read(field, shift):
            where = pl.ds(t + (field * ext + shift), RIM)
            return flat_ref[where, :], side_ref[where, :]

        ground, rough = read(GROUND, 0), read(ROUGH, 0)
        ground_north, rough_north = read(GROUND, 1), read(ROUGH, 1)
        ground_east, rough_east = pair_east(*ground), pair_east(*rough)
        weight = GRAVITY * TIME_STEP
        for j in range(2):
            fixed_ref[j, 0, at, :] = jnp.maximum(ground[j], ground_east[j])
            fixed_ref[j, 1, at, :] = weight * (rough[j] * rough_east[j])
            fixed_ref[j, 2, at, :] = jnp.maximum(ground[j], ground_north[j])
            fixed_ref[j, 3, at, :] = weight * (rough[j] * rough_north[j])

    def north_flow(j, t, here, step):
        at = pl.ds(t, RIM)
        north = (own_ref, side_ref)[j][pl.ds(t + 1, RIM), :]
        top = fixed_ref[j, 2, at, :]
        if step == 0:
            flow = first_face(here, north, top, drive)
        else:
            flow = face(flow_ref[j, 1, at, :], here, north, top, drive, fixed_ref[j, 3, at, :])
        e = t + row
        return jnp.where((e == edge_south) | (e == edge_north), 0.0, flow)

    def flows(t, step):
        at = pl.ds(t, RIM)
        final = step == STEPS - 1
        here = own_ref[at, :], side_ref[at, :]
        for j in range(1 if final else 2):
            flow_ref[j, 1, at, :] = north_flow(j, t, here[j], step)
        if final and t == 0:
            return
        east = pair_east(*here)
        for j in range(2):
            top = fixed_ref[j, 0, at, :]
            if step == 0:
                flow = first_face(here[j], east[j], top, drive)
            else:
                flow = face(
                    flow_ref[j, 0, at, :], here[j], east[j], top, drive, fixed_ref[j, 1, at, :]
                )
            flow_ref[j, 0, at, :] = flow

    def update(t, before, step):
        at = pl.ds(t, RIM)
        final = step == STEPS - 1
        to_east = flow_ref[0, 0, at, :], flow_ref[1, 0, at, :]
        west = pair_west(*to_east)
        after = []
        for j in range(1 if final else 2):
            to_north = flow_ref[j, 1, at, :]
            turned = pltpu.roll(to_north, 1, 0)
            south = jnp.where(first_row, before[j], turned)
            after.append(turned)
            moved = share * (west[j] - to_east[j] + south - to_north)
            if final:
                out = pl.ds(t - RIM, RIM)
                new = own_ref[at, :] + moved + gains[0, at, :]
                depth_ref[out, :] = new - flat_ref[pl.ds(t + GROUND * ext, RIM), :]
            elif j == 0:
                own_ref[at, :] = own_ref[at, :] + moved + gains[0, at, :]
            else:
                beside = pl.ds(apart + t, RIM)
                gain = jnp.where(low, gains[0, beside, :], gains[1, beside, :])
                side_ref[at, :] = side_ref[at, :] + moved + gain
        return after

    sent = []

    def send(source, target):
        copy = pltpu.make_async_copy(source, target, out_sems.at[len(sent)])
        copy.start()
        sent.append(copy)

    def update_all(step):
        if step == STEPS - 1:
            before = (pltpu.roll(flow_ref[0, 1, 0:RIM, :], 1, 0),)
            tiles = range(RIM, tail, RIM)
        else:
            before = (zero, zero)
            tiles = range(0, ext, RIM)
        for t in tiles:
            before = update(t, before, step)
            if step == STEPS - 1 and t % (rows // 2) == 0:
                done = pl.ds(t - rows // 2, rows // 2)
                send(depth_ref.at[done, :], depth_out.at[done, :])

    def settle():
        river_ref[0:rows, :] = level_ref[0:rows, :]
        for i in range(slots):
            own = jnp.minimum(list_smem[4, first + i] - RIM, rows)
            other = total + min(i, few)
            river_ref[pl.ds(own, 1), :] = jnp.where(
                crowded[:1], state[LEVEL, i : i + 1, :], state[LEVEL, other : other + 1, :]
            )
        for t in range(0, rows, RIM):
            at = pl.ds(t, RIM)
            ground = flat_ref[pl.ds(t + (GROUND * ext + RIM), RIM), :]
            bed = ground - (1.0 + 0.5 * bank_ref[at, :].astype(jnp.float32))
            river_ref[at, :] = river_ref[at, :] - bed

    for t in range(0, ext, RIM):
        constants_of(t)
        flows(t, 0)
    update_all(0)
    for step in range(1, STEPS):
        final = step == STEPS - 1
        draw()

        running = [reaches(0, total, alive[0]), reaches(total, few + RIM, alive[1])]
        tiles = list(range(0, tail if final else ext, RIM))
        share_of = -(-len(tiles) // SUB)
        for substep in range(SUB):
            for reach in running:
                next(reach)
            for t in tiles[substep * share_of : (substep + 1) * share_of]:
                flows(t, step)
        for reach in running:
            next(reach, None)
        if final:
            own_rows = pl.ds(RIM, rows)
            send(flow_ref.at[0, 0, own_rows, :], east_out)
            send(flow_ref.at[0, 1, own_rows, :], north_out)
        spread()
        if final:
            settle()
            send(river_ref.at[pl.ds(0, rows), :], river_out)
        update_all(step)
    for copy in sent:
        copy.wait()


def swaps(count, first):
    pairs = [(i, i + 1) for i in range(first, count - 1, 2)]
    return pairs + [(b, a) for a, b in pairs]


def body(depth_init, ground, roughness, river_init, reach_mask, width_class, bank_class):
    rows, cols = ground.shape
    slots = rows // 4
    f32 = jnp.float32
    lon_total, lat_total = lax.axis_size("lon"), lax.axis_size("lat")
    mask = reach_mask.reshape(rows)
    vmem = pl.BlockSpec(memory_space=pltpu.VMEM)
    fields = (depth_init, ground, roughness, river_init, width_class, bank_class)
    ext, total = rows + 2 * RIM, slots + RIM
    used = FLOOD_FIELDS * ext + SLOT_FIELDS * total + RIM
    groups = cols // COLS
    message = -(-(used // RIM + slots // COLS) // groups) * RIM
    room = message * groups
    params = pltpu.CompilerParams(vmem_limit_bytes=48 * 1024 * 1024)

    hbm = pl.BlockSpec(memory_space=pltpu.HBM)
    rim_shape = jax.ShapeDtypeStruct((7 * RIM, cols), f32)
    to_p, to_q = pl.pallas_call(
        rows_kernel,
        in_specs=[hbm] * 7,
        out_specs=[vmem, vmem],
        out_shape=[rim_shape, rim_shape],
        scratch_shapes=[
            pltpu.VMEM((2, 4, RIM, cols), f32),
            pltpu.VMEM((2, 2, RIM, cols), jnp.int32),
            pltpu.SMEM((rows,), jnp.int32),
            pltpu.SemaphoreType.DMA((13,)),
        ],
        compiler_params=pltpu.CompilerParams(vmem_limit_bytes=63 * 1024 * 1024),
        name="rims",
    )(mask, *fields)
    got_p = lax.ppermute(to_p, "lat", swaps(lat_total, 0))
    got_q = lax.ppermute(to_q, "lat", swaps(lat_total, 1))
    flat_shape = jax.ShapeDtypeStruct((room, cols), f32)
    own_flat, level, listed = pl.pallas_call(
        own_kernel,
        in_specs=[pl.BlockSpec(memory_space=pl.ANY)] + [vmem] * 6,
        out_specs=[vmem] * 3,
        out_shape=[
            flat_shape,
            jax.ShapeDtypeStruct((rows + RIM, cols), f32),
            jax.ShapeDtypeStruct((RIM, cols), f32),
        ],
        scratch_shapes=[pltpu.VMEM((rows + RIM, cols), f32)] * 2
        + [
            pltpu.SMEM((rows,), jnp.int32),
            pltpu.SMEM((2 * slots,), jnp.int32),
            pltpu.SemaphoreType.DMA,
        ],
        compiler_params=params,
        name="own_reaches",
    )(mask, *fields)

    message_shape = jax.ShapeDtypeStruct((message, cols), f32)
    flat, to_a, to_b = pl.pallas_call(
        functools.partial(pack_kernel, rows),
        in_specs=[vmem] * 4,
        out_specs=[vmem] * 3,
        out_shape=[flat_shape, message_shape, message_shape],
        input_output_aliases={0: 0},
        compiler_params=params,
        name="pack",
    )(own_flat, listed, got_p, got_q)
    ring = swaps(lon_total, 1) + [(lon_total - 1, 0), (0, lon_total - 1)]
    got_a = lax.ppermute(to_a, "lon", swaps(lon_total, 0))
    got_b = lax.ppermute(to_b, "lon", ring)

    tile = jax.ShapeDtypeStruct((rows, cols), f32)
    return pl.pallas_call(
        step_kernel,
        in_specs=[vmem] * 6,
        out_specs=[pl.BlockSpec(memory_space=pl.ANY)] * 4,
        out_shape=[tile] * 4,
        scratch_shapes=[
            pltpu.VMEM((ext + RIM + room, cols), f32),
            pltpu.VMEM((WATER + 1, total + slots // 4 + RIM, cols), f32),
            pltpu.VMEM((2, 2 * (ext + RIM), cols), f32),
            pltpu.VMEM((2, 2, ext, cols), f32),
            pltpu.VMEM((2, 4, ext, cols), f32),
            pltpu.VMEM((rows + RIM, cols), f32),
            pltpu.VMEM((5, RIM, cols), jnp.int32),
            pltpu.SMEM((5, cols), jnp.int32),
            pltpu.VMEM((rows, cols), f32),
            pltpu.SemaphoreType.DMA((5,)),
            pltpu.SemaphoreType.DMA((5,)),
        ],
        compiler_params=params,
        name="steps",
    )(flat, level, bank_class, listed, got_a, got_b)


def solution(mesh):
    grid = P("lat", "lon")
    return jax.shard_map(
        body,
        mesh=mesh,
        in_specs=(grid,) * 7,
        out_specs=(grid,) * 4,
        check_vma=False,
    )
```

```python
import functools

import jax
import jax.numpy as jnp
from jax import lax
from jax.experimental import pallas as pl
from jax.experimental.pallas import tpu as pltpu
from jax.sharding import PartitionSpec as P

SUB = 8
STEPS = 4

GRAVITY = 9.81
CELL_SIZE = 90.0
TIME_STEP = 10.0
SHALLOW = 0.1
EXCHANGE = 0.01
CHANNEL_MANNING = 0.035

RIM = 8
COLS = SUB * (STEPS - 2)
DURATION = TIME_STEP / SUB
SURFACE, GROUND, ROUGH = range(3)
FLOOD_FIELDS = 3
LEVEL, FLUX, BED, WIDTH, GAIN = range(5)
SLOT_FIELDS = 5
TOP, DRIVE, FRICTION, FEED, WATER = range(5, 10)
ROWS_AT_ONCE = 64
TILES_AT_ONCE = 34
UNPACK_AT_ONCE = 20


def lanes(shape):
    return lax.broadcasted_iota(jnp.int32, shape, 1)


def sublanes(shape):
    return lax.broadcasted_iota(jnp.int32, shape, 0)


def east_of(field):
    return pltpu.roll(field, field.shape[1] - 1, 1)


def face(flow, here, there, top, drive, friction):
    height = jnp.maximum(here, there) - top
    driven = flow - drive * height * (there - here)
    spread = jnp.exp(jnp.log(height * height + SHALLOW * SHALLOW) * (-7.0 / 6.0))
    resisted = 1.0 + friction * jnp.abs(flow) * spread
    return driven * pl.reciprocal(resisted, approx=True)


def first_face(here, there, top, drive):
    height = jnp.maximum(here, there) - top
    return -(drive * height * (there - here))


def reach_constants(bed, width):
    top = jnp.maximum(bed, east_of(bed))
    breadth = 0.5 * (width + east_of(width))
    inner = lanes(bed.shape) < bed.shape[1] - 1
    drive = jnp.where(inner, (GRAVITY * DURATION / CELL_SIZE) * breadth, 0.0)
    friction = jnp.where(
        inner, (GRAVITY * DURATION * CHANNEL_MANNING * CHANNEL_MANNING) / breadth, 0.0
    )
    feed = (DURATION / CELL_SIZE) / width
    return top, drive, friction, feed


def west_of(field):
    return pltpu.roll(field, 1, 1)


def advanced(level, west, flux, surface, feed):
    transfer = (EXCHANGE * DURATION) * (level - surface)
    return level + ((west - flux) * feed - transfer), transfer


def first_reaches(level, surface, constants):
    feed = constants[3]
    faces = constants[:3]
    far_east = [east_of(value) for value in faces]
    near_west = [west_of(value) for value in faces]
    far_west = [west_of(value) for value in near_west]
    feeds = west_of(feed), feed, east_of(feed)
    waters = west_of(surface), surface, east_of(surface)
    west = flux = gathered = None
    for pair in range(SUB // 2):
        levels = [west_of(level), level, east_of(level)]
        around = [pltpu.roll(level, 2, 1)] + levels + [pltpu.roll(level, level.shape[1] - 2, 1)]
        if pair:
            flows = [west_of(west), west, flux, east_of(flux)]
        else:
            flows = [None] * 4
        sets = [far_west, near_west, faces, far_east]
        for k in range(4):
            if pair:
                flows[k] = face(flows[k], around[k], around[k + 1], *sets[k])
            else:
                flows[k] = first_face(around[k], around[k + 1], *sets[k][:2])
        for k in range(3):
            levels[k], transfer = advanced(levels[k], flows[k], flows[k + 1], waters[k], feeds[k])
            if k == 1:
                gathered = transfer if gathered is None else gathered + transfer
        west = face(flows[1], levels[0], levels[1], *near_west)
        flux = face(flows[2], levels[1], levels[2], *faces)
        level, transfer = advanced(levels[1], west, flux, surface, feed)
        gathered = gathered + transfer
    return level, flux, gathered


def odd_position(axis):
    return lax.rem(lax.axis_index(axis), 2)


def repeated(count, unroll, step, carry):
    if unroll >= count:
        for i in range(count):
            carry = step(i, carry)
        return carry

    def some(block, carry):
        for j in range(unroll):
            carry = step(block * unroll + j, carry)
        return carry

    return lax.fori_loop(0, count // unroll, some, carry)


def each_row(count, visit, unroll=ROWS_AT_ONCE):
    repeated(count, unroll, lambda i, carry: (visit(i), carry)[1], 0)


def row_of(tile):
    return tile * RIM if isinstance(tile, int) else pl.multiple_of(tile * RIM, RIM)


def each_tile(count, visit, unroll):
    repeated(count, unroll, lambda i, carry: (visit(row_of(i)), carry)[1], 0)


def rows_kernel(mask_hbm, *refs):
    fields, outs, (reals, classes, mask_ref, sems) = refs[:6], refs[6:8], refs[8:]
    rows = mask_hbm.shape[0]
    northern = odd_position("lat") == 0
    copies = [pltpu.make_async_copy(mask_hbm, mask_ref, sems.at[0])]
    for k, field in enumerate(fields):
        for side, start in enumerate((0, rows - RIM)):
            to = reals.at[side, k] if k < 4 else classes.at[side, k - 4]
            copies.append(
                pltpu.make_async_copy(field.at[pl.ds(start, RIM)], to, sems.at[1 + 2 * k + side])
            )
    for copy in copies:
        copy.start()
    for copy in copies:
        copy.wait()
    shape = reals.shape[2:]
    row = sublanes(shape)

    def rims(side, start):
        depth, ground, rough, river = [reals[side, k] for k in range(4)]
        width, bank = classes[side, 0], classes[side, 1]
        live = jnp.zeros(shape, jnp.float32)
        for j in range(RIM):
            live = jnp.where(row == j, mask_ref[start + j].astype(jnp.float32), live)
        bed = ground - (1.0 + 0.5 * bank.astype(jnp.float32))
        wide = 8.0 + 9.0 * width.astype(jnp.float32)
        return [ground + depth, ground, rough, bed + river, bed, wide, live]

    for k, (low, high) in enumerate(zip(rims(0, 0), rims(1, rows - RIM))):
        outs[0][RIM * k : RIM * (k + 1), :] = jnp.where(northern, high, low)
        outs[1][RIM * k : RIM * (k + 1), :] = jnp.where(northern, low, high)


def fill_list(mask_ref, rows_ref):
    rows = mask_ref.shape[0]
    room = rows // 4
    beyond = rows + 2 * RIM
    batch = 16

    for i in range(room):
        rows_ref[i] = beyond
    count = jnp.int32(0)
    for first in range(0, rows, batch):
        bits = [mask_ref[first + j] for j in range(batch)]
        places = []
        for bit in bits:
            places.append(count)
            count = count + bit
        for j, place in enumerate(places):
            rows_ref[place] = first + j + RIM
    rows_ref[count] = beyond
    return count


def own_kernel(
    mask_any, depth_ref, ground_ref, rough_ref, river_ref, width_ref, bank_ref,
    flat_ref, level_ref, listed_ref,
    bed_ref, wide_ref, mask_ref, rows_ref, sem,
):
    rows, cols = depth_ref.shape
    slots = rows // 4
    tail, ext, total = rows + RIM, rows + 2 * RIM, slots + RIM
    base = FLOOD_FIELDS * ext
    fetch = pltpu.make_async_copy(mask_any, mask_ref, sem)
    fetch.start()

    def prepare(t):
        at = pl.ds(t, RIM)
        ground = ground_ref[at, :]
        bed = ground - (1.0 + 0.5 * bank_ref[at, :].astype(jnp.float32))
        flat_ref[pl.ds(t + (SURFACE * ext + RIM), RIM), :] = ground + depth_ref[at, :]
        flat_ref[pl.ds(t + (GROUND * ext + RIM), RIM), :] = ground
        flat_ref[pl.ds(t + (ROUGH * ext + RIM), RIM), :] = rough_ref[at, :]
        level_ref[at, :] = bed + river_ref[at, :]
        bed_ref[at, :] = bed
        wide_ref[at, :] = 8.0 + 9.0 * width_ref[at, :].astype(jnp.float32)

    each_tile(rows // RIM, prepare, TILES_AT_ONCE)
    zero = jnp.zeros((RIM, cols), jnp.float32)
    flat_ref[SURFACE * ext + tail : (SURFACE + 1) * ext, :] = zero
    level_ref[rows:tail, :] = zero
    bed_ref[rows:tail, :] = zero
    wide_ref[rows:tail, :] = zero + 1.0
    lane = lanes((RIM, cols))
    fetch.wait()
    count = fill_list(mask_ref, rows_ref)

    listed = zero + count.astype(jnp.float32)
    for i in range(slots):
        e = rows_ref[i]
        own = jnp.minimum(e - RIM, rows)
        listed = jnp.where(lane == cols - slots + i, e.astype(jnp.float32), listed)
        to = base + i
        of, surface = pl.ds(own, 1), pl.ds(own + (SURFACE * ext + RIM), 1)
        flat_ref[pl.ds(to + LEVEL * total, 1), :] = level_ref[of, :]
        flat_ref[pl.ds(to + BED * total, 1), :] = bed_ref[of, :]
        flat_ref[pl.ds(to + WIDTH * total, 1), :] = wide_ref[of, :]
        flat_ref[pl.ds(to + GAIN * total, 1), :] = flat_ref[surface, :]
    listed_ref[...] = listed

    def part(field):
        return slice(base + field * total, base + field * total + slots)

    width = flat_ref[part(WIDTH), :]
    level, flux, gathered = first_reaches(
        flat_ref[part(LEVEL), :],
        flat_ref[part(GAIN), :],
        reach_constants(flat_ref[part(BED), :], width),
    )
    flat_ref[part(LEVEL), :] = level
    flat_ref[part(FLUX), :] = flux
    flat_ref[part(GAIN), :] = gathered * (width / CELL_SIZE)


def pack_kernel(rows, own_flat, listed_ref, p_ref, q_ref, flat_ref, a_ref, b_ref):
    del own_flat
    cols = a_ref.shape[1]
    ext = rows + 2 * RIM
    slots = rows // 4
    tail, total = rows + RIM, slots + RIM
    base = FLOOD_FIELDS * ext
    half = RIM // 2
    northern = odd_position("lat") == 0
    p, q = p_ref[...], q_ref[...]
    north = jnp.where(northern, p, q)
    south = jnp.where(northern, q, p)

    def rim(block, k):
        return block[RIM * k : RIM * (k + 1)]

    def ends(k):
        return jnp.concatenate([rim(south, k)[half:], rim(north, k)[:half]], axis=0)

    def part(field):
        start = base + field * total + slots
        return slice(start, start + RIM)

    bed, width = ends(4), ends(5)
    level, flux, gathered = first_reaches(ends(3), ends(0), reach_constants(bed, width))
    gained = jnp.where(ends(6) > 0.0, gathered * (width / CELL_SIZE), 0.0)
    for field, value in (
        (LEVEL, level), (FLUX, flux), (BED, bed), (WIDTH, width), (GAIN, gained),
    ):
        flat_ref[part(field), :] = value
    live = base + SLOT_FIELDS * total
    flat_ref[live : live + RIM, :] = ends(6)
    for k in range(FLOOD_FIELDS):
        flat_ref[k * ext : k * ext + RIM, :] = rim(south, k)
        flat_ref[k * ext + tail : (k + 1) * ext, :] = rim(north, k)

    groups = cols // COLS
    group = lanes((RIM, cols)) // COLS
    eastern = odd_position("lon") == 0
    tiles = (base + SLOT_FIELDS * total) // RIM + 1
    listed = listed_ref[...]

    def pack(m, used):
        block_west, block_east = listed, pltpu.roll(listed, cols - COLS, 1)
        for g in range(used):
            source = flat_ref[pl.ds(row_of(m * groups + g), RIM), :]
            moved = pltpu.roll(source, COLS * g, 1) if g else source
            block_west = jnp.where(group == g, moved, block_west)
            block_east = jnp.where(group == (g - 1) % groups, moved, block_east)
        to = pl.ds(row_of(m), RIM)
        a_ref[to, :] = jnp.where(eastern, block_east, block_west)
        b_ref[to, :] = jnp.where(eastern, block_west, block_east)

    each_row(tiles // groups, lambda m: pack(m, groups), UNPACK_AT_ONCE)
    pack(tiles // groups, tiles % groups)


def step_kernel(
    flat_ref, level_ref, bank_ref, listed_ref, a_ref, b_ref,
    depth_out, river_out, east_out, north_out,
    both_ref, state, gains,
    flow_ref, fixed_ref, river_ref, list_rows, list_smem, depth_ref, sems, out_sems,
):
    rows, cols = depth_out.shape
    slots = rows // 4
    tail, ext, total = rows + RIM, rows + 2 * RIM, slots + RIM
    base = FLOOD_FIELDS * ext
    half = RIM // 2
    lat_number, lat_total = lax.axis_index("lat"), lax.axis_size("lat")
    eastern = odd_position("lon") == 0
    lists = a_ref.shape[0] - RIM
    zero = jnp.zeros((RIM, cols), jnp.float32)

    few = slots // 4
    apart = ext + RIM
    own_ref = both_ref.at[pl.ds(0, apart), :]
    side_ref = both_ref.at[pl.ds(apart, both_ref.shape[0] - apart), :]

    own_list = listed_ref[...]
    crowded = jnp.broadcast_to(own_list[:, 0:1], own_list.shape) > few + 0.5
    list_a, list_b = a_ref[lists : lists + RIM, :], b_ref[lists : lists + RIM, :]
    east_list = jnp.where(eastern, list_a, list_b) + apart
    west_list = pltpu.roll(jnp.where(eastern, list_b, list_a), COLS, 1) + apart
    copies = []
    for k, rows_of in enumerate((
        jnp.where(crowded, own_list, east_list), jnp.where(crowded, own_list, west_list),
        jnp.where(crowded, east_list, own_list), jnp.where(crowded, west_list, own_list),
        own_list,
    )):
        list_rows[k] = rows_of.astype(jnp.int32)
        copies.append(pltpu.make_async_copy(list_rows.at[k, 0], list_smem.at[k], sems.at[k]))
        copies[k].start()

    groups = cols // COLS
    lane = lanes((RIM, cols))
    low = lane < cols // 2
    group = lane // COLS

    def unpack(m):
        at = pl.ds(row_of(m), RIM)
        block_a, block_b = a_ref[at, :], b_ref[at, :]
        from_east = jnp.where(eastern, block_a, block_b)
        from_west = jnp.where(eastern, block_b, block_a)
        for g in range(groups):
            both = jnp.where(group == g, from_east, from_west)
            to = pl.ds(row_of(m * groups + g), RIM)
            side_ref[to, :] = pltpu.roll(both, cols - COLS * g, 1) if g else both

    each_row(a_ref.shape[0] // RIM, unpack, UNPACK_AT_ONCE)

    def copy_in(t):
        at, beside = pl.ds(t, RIM), pl.ds(apart + t, RIM)
        own_ref[at, :] = flat_ref[at, :]
        for k in range(2):
            gains[k, at, :] = zero
            gains[k, beside, :] = zero

    each_tile(ext // RIM, copy_in, TILES_AT_ONCE)
    own_ref[ext : ext + RIM, :] = zero

    def chosen(own, side):
        return jnp.where(crowded, own, side), jnp.where(crowded, side, own)

    for t in range(0, total, RIM):
        pairs = []
        for field in range(SLOT_FIELDS):
            at = pl.ds(base + field * total + t, RIM)
            pairs.append(chosen(flat_ref[at, :], side_ref[at, :]))
        for j in range(2):
            to = t
            if j == 1:
                if few <= t < slots:
                    continue
                to = total + min(t, few)
            constants = reach_constants(pairs[BED][j], pairs[WIDTH][j])
            for field, pair in enumerate(pairs):
                state[field, to : to + RIM, :] = pair[j]
            for field, value in zip((TOP, DRIVE, FRICTION, FEED), constants):
                state[field, to : to + RIM, :] = value
    at = pl.ds(base + SLOT_FIELDS * total, RIM)
    alive = [value > 0.0 for value in chosen(flat_ref[at, :], side_ref[at, :])]
    for copy in copies:
        copy.wait()
    first = cols - slots
    places = [(i, list_smem.at[0], list_smem.at[1], first + i) for i in range(slots)]
    places += [(total + i, list_smem.at[2], list_smem.at[3], first + i) for i in range(few)]
    edge = total + few

    def spread():
        for slot, lows, highs, i in places:
            line = state[GAIN, slot : slot + 1, :]
            gains[0, pl.ds(lows[i], 1), :] = line
            gains[1, pl.ds(highs[i], 1), :] = line
        for j, lines in enumerate(
            chosen(state[GAIN, slots:total, :], state[GAIN, edge : edge + RIM, :])
        ):
            for k in range(2):
                start = j * apart
                gains[k, start + half : start + RIM, :] = lines[:half]
                gains[k, start + tail : start + tail + half, :] = lines[half:]

    middle = lanes((1, cols)) < cols // 2

    def draw():
        for slot, lows, highs, i in places:
            state[WATER, slot : slot + 1, :] = jnp.where(
                middle, both_ref[pl.ds(lows[i], 1), :], both_ref[pl.ds(highs[i], 1), :]
            )
        ends = [
            jnp.concatenate([ref[half:RIM, :], ref[tail : tail + half, :]], axis=0)
            for ref in (own_ref, side_ref)
        ]
        for start, value in zip((slots, edge), chosen(*ends)):
            state[WATER, start : start + RIM, :] = value

    spread()

    def reaches(start, size, live):
        at = slice(start, start + size)

        faces = [state[k, at, :] for k in (TOP, DRIVE, FRICTION)]
        west_faces = [west_of(value) for value in faces]
        surface, feed = state[WATER, at, :], state[FEED, at, :]

        level, flux = state[LEVEL, at, :], state[FLUX, at, :]
        west, gathered = west_of(flux), jnp.zeros_like(level)
        for _ in range(SUB):
            west = face(west, west_of(level), level, *west_faces)
            flux = face(flux, level, east_of(level), *faces)
            level, transfer = advanced(level, west, flux, surface, feed)
            gathered = gathered + transfer
            yield
        state[LEVEL, at, :] = level
        state[FLUX, at, :] = flux
        gained = gathered * (state[WIDTH, at, :] / CELL_SIZE)
        fixed = size - RIM
        state[GAIN, start : start + fixed, :] = gained[:fixed]
        state[GAIN, start + fixed : start + size, :] = jnp.where(live, gained[fixed:], 0.0)

    last_lane = lane == cols - 1
    first_lane = lane == 0
    row = sublanes((RIM, cols))
    first_row = row == 0
    drive = GRAVITY * TIME_STEP / CELL_SIZE
    share = TIME_STEP / CELL_SIZE
    edge_south = jnp.where(lat_number == 0, RIM - 1, -1)
    edge_north = jnp.where(lat_number == lat_total - 1, tail - 1, -1)

    def pair_east(own, side):
        a, b = east_of(own), east_of(side)
        return jnp.where(last_lane, b, a), jnp.where(last_lane, a, b)

    def pair_west(own, side):
        a, b = pltpu.roll(own, 1, 1), pltpu.roll(side, 1, 1)
        return jnp.where(first_lane, b, a), jnp.where(first_lane, a, b)

    def constants_of(t):
        at = pl.ds(t, RIM)

        def read(field, shift):
            where = pl.ds(t + (field * ext + shift), RIM)
            return flat_ref[where, :], side_ref[where, :]

        ground, rough = read(GROUND, 0), read(ROUGH, 0)
        ground_north, rough_north = read(GROUND, 1), read(ROUGH, 1)
        ground_east, rough_east = pair_east(*ground), pair_east(*rough)
        weight = GRAVITY * TIME_STEP
        for j in range(2):
            fixed_ref[j, 0, at, :] = jnp.maximum(ground[j], ground_east[j])
            fixed_ref[j, 1, at, :] = weight * (rough[j] * rough_east[j])
            fixed_ref[j, 2, at, :] = jnp.maximum(ground[j], ground_north[j])
            fixed_ref[j, 3, at, :] = weight * (rough[j] * rough_north[j])

    def north_flow(j, t, here, step):
        at = pl.ds(t, RIM)
        north = (own_ref, side_ref)[j][pl.ds(t + 1, RIM), :]
        top = fixed_ref[j, 2, at, :]
        if step == 0:
            flow = first_face(here, north, top, drive)
        else:
            flow = face(flow_ref[j, 1, at, :], here, north, top, drive, fixed_ref[j, 3, at, :])
        e = t + row
        return jnp.where((e == edge_south) | (e == edge_north), 0.0, flow)

    def flows(t, step):
        at = pl.ds(t, RIM)
        final = step == STEPS - 1
        here = own_ref[at, :], side_ref[at, :]
        for j in range(1 if final else 2):
            flow_ref[j, 1, at, :] = north_flow(j, t, here[j], step)
        if final and t == 0:
            return
        east = pair_east(*here)
        for j in range(2):
            top = fixed_ref[j, 0, at, :]
            if step == 0:
                flow = first_face(here[j], east[j], top, drive)
            else:
                flow = face(
                    flow_ref[j, 0, at, :], here[j], east[j], top, drive, fixed_ref[j, 1, at, :]
                )
            flow_ref[j, 0, at, :] = flow

    def update(t, before, step):
        at = pl.ds(t, RIM)
        final = step == STEPS - 1
        to_east = flow_ref[0, 0, at, :], flow_ref[1, 0, at, :]
        west = pair_west(*to_east)
        after = []
        for j in range(1 if final else 2):
            to_north = flow_ref[j, 1, at, :]
            turned = pltpu.roll(to_north, 1, 0)
            south = jnp.where(first_row, before[j], turned)
            after.append(turned)
            moved = share * (west[j] - to_east[j] + south - to_north)
            if final:
                out = pl.ds(t - RIM, RIM)
                new = own_ref[at, :] + moved + gains[0, at, :]
                depth_ref[out, :] = new - flat_ref[pl.ds(t + GROUND * ext, RIM), :]
            elif j == 0:
                own_ref[at, :] = own_ref[at, :] + moved + gains[0, at, :]
            else:
                beside = pl.ds(apart + t, RIM)
                gain = jnp.where(low, gains[0, beside, :], gains[1, beside, :])
                side_ref[at, :] = side_ref[at, :] + moved + gain
        return after

    sent = []

    def send(source, target):
        copy = pltpu.make_async_copy(source, target, out_sems.at[len(sent)])
        copy.start()
        sent.append(copy)

    def update_all(step):
        if step == STEPS - 1:
            before = (pltpu.roll(flow_ref[0, 1, 0:RIM, :], 1, 0),)
            tiles = range(RIM, tail, RIM)
        else:
            before = (zero, zero)
            tiles = range(0, ext, RIM)
        for t in tiles:
            before = update(t, before, step)
            if step == STEPS - 1 and t % (rows // 2) == 0:
                done = pl.ds(t - rows // 2, rows // 2)
                send(depth_ref.at[done, :], depth_out.at[done, :])

    def settle():
        river_ref[0:rows, :] = level_ref[0:rows, :]
        for i in range(slots):
            own = jnp.minimum(list_smem[4, first + i] - RIM, rows)
            other = total + min(i, few)
            river_ref[pl.ds(own, 1), :] = jnp.where(
                crowded[:1], state[LEVEL, i : i + 1, :], state[LEVEL, other : other + 1, :]
            )
        for t in range(0, rows, RIM):
            at = pl.ds(t, RIM)
            ground = flat_ref[pl.ds(t + (GROUND * ext + RIM), RIM), :]
            bed = ground - (1.0 + 0.5 * bank_ref[at, :].astype(jnp.float32))
            river_ref[at, :] = river_ref[at, :] - bed

    for t in range(0, ext, RIM):
        constants_of(t)
        flows(t, 0)
    update_all(0)
    for step in range(1, STEPS):
        final = step == STEPS - 1
        draw()

        running = [reaches(0, total, alive[0]), reaches(total, few + RIM, alive[1])]
        tiles = list(range(0, tail if final else ext, RIM))
        share_of = -(-len(tiles) // SUB)
        for substep in range(SUB):
            for reach in running:
                next(reach)
            for t in tiles[substep * share_of : (substep + 1) * share_of]:
                flows(t, step)
        for reach in running:
            next(reach, None)
        if final:
            own_rows = pl.ds(RIM, rows)
            send(flow_ref.at[0, 0, own_rows, :], east_out)
            send(flow_ref.at[0, 1, own_rows, :], north_out)
        spread()
        if final:
            settle()
            send(river_ref.at[pl.ds(0, rows), :], river_out)
        update_all(step)
    for copy in sent:
        copy.wait()


def swaps(count, first):
    pairs = [(i, i + 1) for i in range(first, count - 1, 2)]
    return pairs + [(b, a) for a, b in pairs]


def body(depth_init, ground, roughness, river_init, reach_mask, width_class, bank_class):
    rows, cols = ground.shape
    slots = rows // 4
    f32 = jnp.float32
    lon_total, lat_total = lax.axis_size("lon"), lax.axis_size("lat")
    mask = reach_mask.reshape(rows)
    vmem = pl.BlockSpec(memory_space=pltpu.VMEM)
    fields = (depth_init, ground, roughness, river_init, width_class, bank_class)
    ext, total = rows + 2 * RIM, slots + RIM
    used = FLOOD_FIELDS * ext + SLOT_FIELDS * total + RIM
    groups = cols // COLS
    message = -(-(used // RIM + slots // COLS) // groups) * RIM
    room = message * groups
    params = pltpu.CompilerParams(vmem_limit_bytes=48 * 1024 * 1024)

    hbm = pl.BlockSpec(memory_space=pltpu.HBM)
    rim_shape = jax.ShapeDtypeStruct((7 * RIM, cols), f32)
    to_p, to_q = pl.pallas_call(
        rows_kernel,
        in_specs=[hbm] * 7,
        out_specs=[vmem, vmem],
        out_shape=[rim_shape, rim_shape],
        scratch_shapes=[
            pltpu.VMEM((2, 4, RIM, cols), f32),
            pltpu.VMEM((2, 2, RIM, cols), jnp.int32),
            pltpu.SMEM((rows,), jnp.int32),
            pltpu.SemaphoreType.DMA((13,)),
        ],
        compiler_params=pltpu.CompilerParams(vmem_limit_bytes=63 * 1024 * 1024),
        name="rims",
    )(mask, *fields)
    got_p = lax.ppermute(to_p, "lat", swaps(lat_total, 0))
    got_q = lax.ppermute(to_q, "lat", swaps(lat_total, 1))
    flat_shape = jax.ShapeDtypeStruct((room, cols), f32)
    own_flat, level, listed = pl.pallas_call(
        own_kernel,
        in_specs=[pl.BlockSpec(memory_space=pl.ANY)] + [vmem] * 6,
        out_specs=[vmem] * 3,
        out_shape=[
            flat_shape,
            jax.ShapeDtypeStruct((rows + RIM, cols), f32),
            jax.ShapeDtypeStruct((RIM, cols), f32),
        ],
        scratch_shapes=[pltpu.VMEM((rows + RIM, cols), f32)] * 2
        + [
            pltpu.SMEM((rows,), jnp.int32),
            pltpu.SMEM((2 * slots,), jnp.int32),
            pltpu.SemaphoreType.DMA,
        ],
        compiler_params=params,
        name="own_reaches",
    )(mask, *fields)

    message_shape = jax.ShapeDtypeStruct((message, cols), f32)
    flat, to_a, to_b = pl.pallas_call(
        functools.partial(pack_kernel, rows),
        in_specs=[vmem] * 4,
        out_specs=[vmem] * 3,
        out_shape=[flat_shape, message_shape, message_shape],
        input_output_aliases={0: 0},
        compiler_params=params,
        name="pack",
    )(own_flat, listed, got_p, got_q)
    ring = swaps(lon_total, 1) + [(lon_total - 1, 0), (0, lon_total - 1)]
    got_a = lax.ppermute(to_a, "lon", swaps(lon_total, 0))
    got_b = lax.ppermute(to_b, "lon", ring)

    tile = jax.ShapeDtypeStruct((rows, cols), f32)
    return pl.pallas_call(
        step_kernel,
        in_specs=[vmem] * 6,
        out_specs=[pl.BlockSpec(memory_space=pl.ANY)] * 4,
        out_shape=[tile] * 4,
        scratch_shapes=[
            pltpu.VMEM((ext + RIM + room, cols), f32),
            pltpu.VMEM((WATER + 1, total + slots // 4 + RIM, cols), f32),
            pltpu.VMEM((2, 2 * (ext + RIM), cols), f32),
            pltpu.VMEM((2, 2, ext, cols), f32),
            pltpu.VMEM((2, 4, ext, cols), f32),
            pltpu.VMEM((rows + RIM, cols), f32),
            pltpu.VMEM((5, RIM, cols), jnp.int32),
            pltpu.SMEM((5, cols), jnp.int32),
            pltpu.VMEM((rows, cols), f32),
            pltpu.SemaphoreType.DMA((5,)),
            pltpu.SemaphoreType.DMA((5,)),
        ],
        compiler_params=params,
        name="steps",
    )(flat, level, bank_class, listed, got_a, got_b)


def solution(mesh):
    grid = P("lat", "lon")
    return jax.shard_map(
        body,
        mesh=mesh,
        in_specs=(grid,) * 7,
        out_specs=(grid,) * 4,
        check_vma=False,
    )
```
